128 devices in a mesh: slot: 16 (over z, x_hi, core), tok: 8 (over y, x_lo).
Axes of the slice: x: 4 (x_hi: 2, x_lo: 2; x = x_hi * 2 + x_lo), y: 4, z: 4, core: 2. Of those that a mesh axis runs over, the one named last changes fastest.
Arguments:
- latents: bfloat16 [16, 1024, 5120], P('slot', 'tok'), may hold values from -3 to 3
- gain: float32 [5120], replicated, may hold values from 0.5 to 1.5
- mod_table: float32 [16, 2, 5120], replicated, may hold values from -3 to 3
- slot_noise_level: int32 [16], P('slot'), may hold values from 0 to 15
- key_block_index: int32 [16, 8, 4], P('slot'), may hold values from 0 to 15
- counts: int32 [16, 8], P('slot'), may hold values from 1 to 4
- w_qkv: bfloat16 [3, 5120, 3072], P(None, 'slot', 'tok')
- w_out: bfloat16 [3072, 5120], P('tok', 'slot'), may hold values from -0.25 to 0.25
Outputs:
- shifted: bfloat16 [16, 1024, 5120], P('slot', 'tok')
The draws below stay inside these ranges and needn't reach their ends.
Inputs may be any that keep to these rules, and one draw needn't show every extreme that they name: `key_block_index`: entries 0 to 7 name the slot's own tiles, 8 to 15 the preceding slot's; only the first counts entries of a list are read, and they may repeat.
All inputs are finite; a program needn't handle non-finite values.
Results may differ from the reference program's by a relative error of at most 0.018.
Values may be sent and summed in bfloat16 or wider, within the bound.
A program may use at most 128 MiB of HBM per device.

```python
import math
import jax
import jax.numpy as jnp
from jax import lax

MODEL_WIDTH = 5120
HEADS = 24
HD = 128
BLK = 128
LISTED_BLOCKS = 4
NOISE_STEPS = 16
FRAME_SLOTS = 16
SLOT_TOKENS = 1024
QUERY_TILES = 8
N_TOK = 8


def draw_latents(key, part):
    key = jax.random.fold_in(key, 11)
    value_rows = jnp.clip(0.5 * jax.random.normal(key, (FRAME_SLOTS, SLOT_TOKENS, MODEL_WIDTH), jnp.float32), -3.0, 3.0)
    return value_rows.astype(jnp.bfloat16)


def draw_w_qkv(key, part):
    key = jax.random.fold_in(key, 23)
    key_base = jax.random.fold_in(key, 0)
    width = HEADS * HD
    base_offset = jnp.clip(jax.random.normal(key_base, (3, MODEL_WIDTH, width), jnp.float32), -4.0, 4.0) * MODEL_WIDTH ** (-0.5)
    return base_offset.astype(jnp.bfloat16)


def set_ends(drawn, key, low, top_value):
    longest = drawn.shape.index(max(drawn.shape))
    spots = []
    for shift in (0, 1):
        where = [jax.random.randint(jax.random.fold_in(key, axis), (), 0, length) for axis, length in enumerate(drawn.shape)]
        where[longest] = (where[longest] + shift) % drawn.shape[longest]
        spots.append(tuple(where))
    return drawn.at[spots[0]].set(low).at[spots[1]].set(top_value)


def shard_levels(stream_key, shape, cuts, least, high):
    factor_of = 1.0
    for dim, shards_of in cuts:
        draws = jax.random.uniform(jax.random.fold_in(jax.random.fold_in(stream_key, 6), dim), (shards_of,), jnp.float32, least / len(cuts), high / len(cuts))
        factor_of = factor_of * jnp.repeat(jnp.exp(draws), shape[dim] // shards_of).reshape((-1,) + (1,) * (len(shape) - 1 - dim))
    return factor_of


def scatter_about(own_key, shape, scale, most, cuts=(), kind=jnp.bfloat16):
    array = jax.random.normal(own_key, shape, jnp.float32) * scale
    if len(cuts) > 0:
        array = shard_levels(own_key, shape, cuts, -0.22, 0.18) * array
    return jnp.clip(array, min=-most, max=most).astype(kind)


def setup_inputs(seed: int = 0) -> dict:
    seeds = jax.random.split(jax.random.key(seed), 9)
    return {
        "latents": draw_latents(jax.random.fold_in(seeds[8], 71), 0),
        "gain": jnp.clip(1.0 + 0.1 * jax.random.normal(seeds[1], (MODEL_WIDTH,), jnp.float32), 0.5, 1.5),
        "mod_table": scatter_about(seeds[2], (NOISE_STEPS, 2, MODEL_WIDTH), 0.5, 3.0, (), jnp.float32),
        "slot_noise_level": set_ends(jax.random.randint(seeds[3], (FRAME_SLOTS,), 0, NOISE_STEPS), jax.random.fold_in(seeds[3], 1), 0, NOISE_STEPS - 1).astype(jnp.int32),
        "key_block_index": set_ends(jax.random.randint(seeds[4], (FRAME_SLOTS, QUERY_TILES, LISTED_BLOCKS), 0, 2 * QUERY_TILES), jax.random.fold_in(seeds[4], 1), 0, (2 * QUERY_TILES) - 1).astype(jnp.int32),
        "counts": set_ends(jax.random.randint(seeds[5], (FRAME_SLOTS, QUERY_TILES), 1, LISTED_BLOCKS + 1), jax.random.fold_in(seeds[5], 1), 1, LISTED_BLOCKS).astype(jnp.int32),
        "w_qkv": draw_w_qkv(jax.random.fold_in(seeds[8], 71), 0),
        "w_out": scatter_about(seeds[7], (HEADS * HD, MODEL_WIDTH), (4 * HD) ** -0.5, 0.25, ((0, 8), (1, 16))),
    }


def tile_allowed(ids, count):
    tiles = ids.shape[0]
    valid = jnp.arange(LISTED_BLOCKS, dtype=jnp.int32)[None, :] < count[:, None]
    hit = (ids[:, :, None] == jnp.arange(2 * tiles, dtype=jnp.int32)[None, None, :]) & valid[:, :, None]
    hit = jnp.any(hit, axis=1)
    return jnp.repeat(jnp.repeat(hit, BLK, axis=0), BLK, axis=1)

def attend(queries, keys, value_rows, allowed):
    rows = queries.shape[0]
    heads = queries.shape[1] // HD
    qh = queries.reshape(rows, heads, HD).transpose(1, 0, 2)
    kh = keys.reshape(keys.shape[0], heads, HD).transpose(1, 0, 2)
    vh = value_rows.reshape(value_rows.shape[0], heads, HD).transpose(1, 0, 2)

    def one_head(items):
        query, key, value = items
        scores = jnp.einsum('qd,kd->qk', query.astype(jnp.float32), key.astype(jnp.float32)) * (1.0 / math.sqrt(HD))
        scores = jnp.where(allowed, scores, -1e+30)
        top = lax.optimization_barrier(jnp.max(scores, axis=1, keepdims=True))
        expo = jnp.exp(scores - top)
        probs = (expo / lax.optimization_barrier(jnp.sum(expo, axis=1, keepdims=True))).astype(jnp.bfloat16)
        return jnp.dot(probs, value, preferred_element_type=jnp.float32).astype(jnp.bfloat16)
    out = lax.map(one_head, (qh, kh, vh))
    return out.transpose(1, 0, 2).reshape(rows, heads * HD)

def reference(latents, gain, mod_table, slot_noise_level, key_block_index, counts, w_qkv, w_out):
    modul = mod_table[slot_noise_level]
    xf = latents.astype(jnp.float32)
    mean = lax.optimization_barrier(jnp.mean(xf, axis=-1, keepdims=True))
    centred = xf - mean
    var = lax.optimization_barrier(jnp.mean(centred * centred, axis=-1, keepdims=True))
    gaussian_sample = centred * lax.rsqrt(var + 1e-06)
    normed = (gaussian_sample * gain * (1.0 + modul[:, 0][:, None, :]) + modul[:, 1][:, None, :]).astype(jnp.bfloat16)
    flat = normed.reshape(-1, normed.shape[2])
    width = w_qkv.shape[2]
    slots = latents.shape[0]
    rows = latents.shape[1]
    proj = [jnp.dot(flat, w_qkv[j], preferred_element_type=jnp.float32).astype(jnp.bfloat16).reshape(slots, rows, width) for j in range(3)]
    queries, keys, value_rows = proj
    ctx_keys = jnp.concatenate([keys, jnp.roll(keys, 1, axis=0)], axis=1)
    ctx_values = jnp.concatenate([value_rows, jnp.roll(value_rows, 1, axis=0)], axis=1)

    def one_slot(items):
        query, key, value, ids, count = items
        return attend(query, key, value, tile_allowed(ids, count))
    attn = lax.map(one_slot, (queries, ctx_keys, ctx_values, key_block_index, counts))
    attn_flat = attn.reshape(-1, width)
    group = width // N_TOK
    branch = jnp.zeros((attn_flat.shape[0], w_out.shape[1]), jnp.float32)
    for g in range(N_TOK):
        part = jnp.dot(attn_flat[:, g * group:(g + 1) * group], w_out[g * group:(g + 1) * group], preferred_element_type=jnp.float32).astype(jnp.bfloat16)
        part = lax.optimization_barrier(part)
        branch = branch + part.astype(jnp.float32)
    updated = (xf + branch.reshape(slots, rows, -1)).astype(jnp.bfloat16)
    return jnp.roll(updated, 1, axis=0)
```

```python
import functools
import math

import jax
import jax.numpy as jnp
from jax import lax
from jax.experimental import pallas as pl
from jax.experimental.pallas import tpu as pltpu
from jax.sharding import PartitionSpec as P

MESH = pl.DeviceIdType.MESH
BF16 = jnp.bfloat16
F32 = jnp.float32

HD = 128
ROWS = 128
D = 5120
QKV = 1152
PIECE = 320
HALF = 64
KCHUNK = 1024
GROUP = 384

NAMES = (
    "w_xh", "w_zp0", "w_zm0", "w_co0", "w_zp1", "w_zm1", "w_co1", "w_fp0", "w_fm0", "w_co2", "w_co3",
    "w_fp1", "w_fm1", "w_co4", "w_co5", "w_co6", "w_co7", "t_x0", "t_x1", "t_yp0", "t_yp1", "t_ym0", "t_ym1",
    "t_fp", "t_fm", "u_yp0", "u_yp1", "u_ym0", "u_ym1", "u_x0", "u_x1", "o_a0", "o_a1", "o_a2", "o_a3",
    "o_xh", "o_zp", "o_zm", "o_co0", "o_fp", "o_fm", "o_co1", "o_co2", "o_co3",
)
SEM = {name: i for i, name in enumerate(NAMES)}
KV0 = len(NAMES)
A_YP = KV0 + 8
A_YM = A_YP + 8
A_FP = A_YM + 8
A_FM = A_FP + 8
P_X = A_FM + 8
S_Y = P_X + 4
OUT = S_Y + 4
N_SEM = OUT + 4


def kernel(lat, gain, mod, level, ids, counts, wq, wo, out,
           x, w, wout, q, ctx, att, acc, psend, precv, ssend, srecv, upd, latc, local, ss, rs):
    s, t = lax.axis_index("slot"), lax.axis_index("tok")
    z, h, c = s // 4, (s // 2) % 2, s % 2
    y, l = t // 2, t % 2

    def slot(zz, hh, cc):
        return (zz % 4) * 4 + hh * 2 + cc

    def tok(yy, ll):
        return (yy % 4) * 2 + ll

    XL = (s, tok(y, 1 - l))
    YP, YM, Y2 = (s, tok(y + 1, l)), (s, tok(y + 3, l)), (s, tok(y + 2, l))
    ZP, ZM = (slot(z + 1, h, c), t), (slot(z + 3, h, c), t)
    XH, CO = (slot(z, 1 - h, c), t), (slot(z, h, 1 - c), t)
    NX, PV = ((s + 1) % 16, t), ((s + 15) % 16, t)

    def copy(src, dst, sem, dev):
        k = SEM[sem] if isinstance(sem, str) else sem
        return pltpu.make_async_remote_copy(
            src_ref=src, dst_ref=dst, send_sem=ss.at[k], recv_sem=rs.at[k], device_id=dev, device_id_type=MESH
        )

    sent = []

    def send(ref, sem, dev):
        cp = copy(ref, ref, sem, dev)
        cp.start()
        sent.append(cp)
        return cp

    barrier = pltpu.get_barrier_semaphore()
    peers = (XL, YP, YM, Y2, ZP, ZM, XH, CO, NX, PV)
    for dev in peers:
        pl.semaphore_signal(barrier, inc=1, device_id=dev, device_id_type=MESH)

    def wrows(piece, first=0, size=PIECE):
        return w.at[pl.ds(pl.multiple_of(piece * PIECE + first, 32), size)]

    own = [
        pltpu.make_async_copy(
            wq.at[j], w.at[pl.ds(pl.multiple_of(s * PIECE, 64), PIECE), pl.ds(j * GROUP, GROUP)], local.at[j]
        )
        for j in range(3)
    ]
    for cp in own:
        cp.start()
    for cp in own:
        cp.wait()
    pl.semaphore_wait(barrier, len(peers))

    mine = wrows(s)
    w_xh = send(mine, "w_xh", XH)
    w_zp0 = send(mine, "w_zp0", ZP)
    w_zm0 = send(mine, "w_zm0", ZM)
    w_co = [send(mine, "w_co0", CO)]

    lv = level[0]
    factor = gain[...] * (1.0 + mod[lv, 0:1, :])
    offset = mod[lv, 1:2, :]

    def norm(i, _):
        rows = pl.ds(pl.multiple_of(i * 16, 16), 16)
        xf = lat[rows, :].astype(F32)
        mean = jnp.mean(xf, axis=-1, keepdims=True)
        centred = xf - mean
        var = jnp.mean(centred * centred, axis=-1, keepdims=True)
        x[t, rows, :] = (centred * lax.rsqrt(var + 1e-06) * factor + offset).astype(BF16)
        return 0

    def shard(tt, half):
        return x.at[tt, pl.ds(half * HALF, HALF)]

    t_x, t_yp, t_ym = [], [], []
    for half in range(2):
        lax.fori_loop(half * 4, half * 4 + 4, norm, 0)
        t_yp.append(send(shard(t, half), "t_yp%d" % half, YP))
        t_ym.append(send(shard(t, half), "t_ym%d" % half, YM))
        t_x.append(send(shard(t, half), "t_x%d" % half, XL))

    yd = h * 2 + c
    gather = y == yd
    active = c == y % 2
    relay = active & (h != y // 2)

    def orows(zz, first, size):
        return wout.at[zz % 4, pl.ds(first, size)]

    def o_first():
        dst = wout.at[z, pl.ds(pl.multiple_of(y * GROUP, 128), GROUP)]
        return copy(wo, dst, SEM["o_a0"] + (y - yd + 4) % 4, (s, tok(yd, l)))

    def o_copy(name, dev):
        zz = {"o_xh": z, "o_zp": z, "o_zm": z, "o_co0": z, "o_fp": z + 3, "o_fm": z + 1, "o_co1": z + 3, "o_co2": z + 1, "o_co3": z + 2}[name]
        if name == "o_fp":
            ref = orows(zz, 0, 768)
        elif name == "o_fm":
            ref = orows(zz, 768, 768)
        else:
            ref = wout.at[zz % 4]
        return copy(ref, ref, name, dev)

    @pl.when(jnp.logical_not(gather))
    def _():
        o_first().start()

    @pl.when(gather)
    def _():
        cp = pltpu.make_async_copy(wo, wout.at[z, pl.ds(pl.multiple_of(y * GROUP, 128), GROUP)], local.at[3])
        cp.start()
        cp.wait()

    for yy in range(4):
        for zz in range(4):
            first = (zz * 4 + yy) * PIECE
            latc[yy, zz] = lat[:, first:first + PIECE]

    tm, tp, tx = tok(y + 3, l), tok(y + 1, l), tok(y, 1 - l)
    t2 = tok(y + 2, l)
    w_xh.wait_recv()
    px = slot(z, 1 - h, c)
    w_zp1 = send(wrows(px), "w_zp1", ZP)
    w_zm1 = send(wrows(px), "w_zm1", ZM)
    w_co.append(send(wrows(px), "w_co1", CO))

    t_yp[0].wait_recv()
    t_fp = send(shard(tm, 0), "t_fp", YP)
    w_zp0.wait_recv()
    pm = slot(z + 3, h, c)
    w_fp0 = send(wrows(pm, 0, PIECE // 2), "w_fp0", ZP)
    w_co.append(send(wrows(pm), "w_co2", CO))
    w_zm0.wait_recv()
    pp = slot(z + 1, h, c)
    w_fm0 = send(wrows(pp, PIECE // 2, PIECE // 2), "w_fm0", ZM)
    w_co.append(send(wrows(pp), "w_co3", CO))
    t_ym[1].wait_recv()
    t_fm = send(shard(tp, 1), "t_fm", YM)

    u_yp, u_ym = [], []
    for half in range(2):
        t_x[half].wait_recv()
        u_yp.append(send(shard(tx, half), "u_yp%d" % half, YP))
        u_ym.append(send(shard(tx, half), "u_ym%d" % half, YM))

    @pl.when(gather)
    def _():
        for d in range(1, 4):
            src = wout.at[z, pl.ds(0, GROUP)]
            copy(src, src, SEM["o_a0"] + d, YP).wait_recv()
        o_copy("o_xh", XH).start()

    w_zp1.wait_recv()
    pm1 = slot(z + 3, 1 - h, c)
    w_fp1 = send(wrows(pm1, 0, PIECE // 2), "w_fp1", ZP)
    w_co.append(send(wrows(pm1), "w_co4", CO))
    w_zm1.wait_recv()
    pp1 = slot(z + 1, 1 - h, c)
    w_fm1 = send(wrows(pp1, PIECE // 2, PIECE // 2), "w_fm1", ZM)
    w_co.append(send(wrows(pp1), "w_co5", CO))

    @pl.when(relay)
    def _():
        o_copy("o_xh", XH).wait_recv()

    @pl.when(active)
    def _():
        o_copy("o_zp", ZP).start()
        o_copy("o_zm", ZM).start()
        o_copy("o_co0", CO).start()

    w_fp0.wait_recv()
    w_fm0.wait_recv()
    w_co.append(send(wrows(slot(z + 2, h, c)), "w_co6", CO))
    t_fp.wait_recv()
    u_x = [send(shard(t2, 0), "u_x0", XL)]
    t_fm.wait_recv()
    u_x.append(send(shard(t2, 1), "u_x1", XL))
    w_fp1.wait_recv()
    w_fm1.wait_recv()
    w_co.append(send(wrows(slot(z + 2, 1 - h, c)), "w_co7", CO))
    for cp in w_co:
        cp.wait_recv()

    kv = {}

    def project(ta, tb, first):
        def step(k, _):
            cols = pl.ds(pl.multiple_of(k * KCHUNK, KCHUNK), KCHUNK)
            rows = jnp.concatenate([x[ta, :, cols], x[tb, :, cols]], axis=0)
            part = jnp.dot(rows, w[cols, :], preferred_element_type=F32)

            @pl.when(k == 0)
            def _():
                acc[...] = part

            @pl.when(k > 0)
            def _():
                acc[...] += part

            return 0

        lax.fori_loop(0, D // KCHUNK, step, 0)
        for i, tt in enumerate((ta, tb)):
            rows = pl.ds(i * ROWS, ROWS)
            ctx[tt] = acc[rows, GROUP:].astype(BF16)
            cp = copy(ctx.at[tt], ctx.at[8 + tt], KV0 + first + i, NX)
            cp.start()
            kv[first + i] = cp
            sent.append(cp)
            q[tt] = acc[rows, :GROUP].astype(BF16)

    project(t, tx, 0)
    t_yp[1].wait_recv()
    t_ym[0].wait_recv()
    project(tm, tp, 2)

    @pl.when(active)
    def _():
        o_copy("o_zp", ZP).wait_recv()
        o_copy("o_fp", ZP).start()
        o_copy("o_co1", CO).start()
        o_copy("o_zm", ZM).wait_recv()
        o_copy("o_fm", ZM).start()
        o_copy("o_co2", CO).start()

    for half in range(2):
        u_yp[half].wait_recv()
        u_ym[half].wait_recv()
    project(tok(y + 3, 1 - l), tok(y + 1, 1 - l), 4)
    u_x[0].wait_recv()
    u_x[1].wait_recv()
    project(t2, tok(y + 2, 1 - l), 6)

    @pl.when(active)
    def _():
        o_copy("o_fp", ZP).wait_recv()
        o_copy("o_fm", ZM).wait_recv()
        o_copy("o_co3", CO).start()

    for k in range(8):
        kv[k].wait_recv()

    scale = 1.0 / math.sqrt(HD)
    ycols = pl.ds(pl.multiple_of(y * GROUP, 128), GROUP)

    def tile_of(k):
        return 2 * (k % 4) + jnp.where(k < 4, 1 - l, l)

    def acols(yy):
        return pl.ds(pl.multiple_of((yy % 4) * GROUP, 128), GROUP)

    def a_copy(k, base):
        i = tile_of(k)
        if base == A_YP:
            ref, dev = att.at[i, :, ycols], YP
        elif base == A_YM:
            ref, dev = att.at[i, :, ycols], YM
        elif base == A_FP:
            ref, dev = att.at[i, pl.ds(0, HALF), acols(y + 3)], YP
        else:
            ref, dev = att.at[i, pl.ds(HALF, HALF), acols(y + 1)], YM
        return copy(ref, ref, base + k, dev)

    def attend(k):
        i = tile_of(k)
        listed = [ids[i, j] for j in range(4)]
        valid = []
        for j in range(4):
            ok = j < counts[i]
            for e in range(j):
                ok = ok & (listed[e] != listed[j])
            valid.append(ok)
        outs = []
        for head in range(3):
            hc = slice(head * HD, (head + 1) * HD)
            vc = slice(GROUP + head * HD, GROUP + (head + 1) * HD)
            query = q[i, :, hc]
            scores = []
            for j in range(4):
                sc = lax.dot_general(
                    query, ctx[listed[j], :, hc], (((1,), (1,)), ((), ())), preferred_element_type=F32
                ) * scale
                scores.append(jnp.where(valid[j], sc, -1e30))
            top = jnp.maximum(jnp.maximum(scores[0], scores[1]), jnp.maximum(scores[2], scores[3]))
            top = jnp.max(top, axis=1, keepdims=True)
            expo = [jnp.exp(sc - top) for sc in scores]
            total = jnp.sum((expo[0] + expo[1]) + (expo[2] + expo[3]), axis=1, keepdims=True)
            probs = jnp.concatenate([(e / total).astype(BF16) for e in expo], axis=1)
            values = jnp.concatenate([ctx[listed[j], :, vc] for j in range(4)], axis=0)
            outs.append(jnp.dot(probs, values, preferred_element_type=F32).astype(BF16))
        att[i, :, ycols] = jnp.concatenate(outs, axis=1)
        a_copy(k, A_YP).start()
        a_copy(k, A_YM).start()

    def forward(k):
        a_copy(k, A_YP).wait_recv()
        a_copy(k, A_FP).start()
        a_copy(k, A_YM).wait_recv()
        a_copy(k, A_FM).start()

    def product(k, zz):
        return jnp.dot(att[tile_of(k)], wout[zz], preferred_element_type=F32)

    def p_copy(k):
        return copy(psend.at[k], precv.at[k], P_X + k, XL)

    def foreign(k):
        a_copy(k, A_FP).wait_recv()
        a_copy(k, A_FM).wait_recv()
        for zz in range(4):
            psend[k, zz] = product(k, zz).astype(BF16)
        p_copy(k).start()

    def s_copy(yt):
        return copy(ssend.at[yt], srecv.at[y], S_Y + (yt - y + 4) % 4, (s, tok(yt, l)))

    def finish(yt):
        k = yt + 4
        a_copy(k, A_FP).wait_recv()
        a_copy(k, A_FM).wait_recv()
        p_copy(yt).wait_recv()
        for zz in range(4):
            ssend[yt, zz] = (product(k, zz) + precv[yt, zz].astype(F32)).astype(BF16)

        @pl.when(yt != y)
        def _():
            s_copy(yt).start()

        @pl.when(yt == y)
        def _():
            srecv[y] = ssend[yt]

    def wait_out_weights():
        @pl.when(jnp.logical_not(active))
        def _():
            for name in ("o_co0", "o_co1", "o_co2", "o_co3"):
                o_copy(name, CO).wait_recv()

    def early(k, _):
        attend(k)

        @pl.when(k >= 2)
        def _():
            forward(k - 2)

        @pl.when(k == 4)
        def _():
            wait_out_weights()

        @pl.when(k >= 4)
        def _():
            foreign(k - 4)

        return 0

    lax.fori_loop(0, 8, early, 0)
    forward(6)
    forward(7)

    def late(yt, _):
        finish(yt)
        return 0

    lax.fori_loop(0, 4, late, 0)

    outs = []
    for yy in range(4):
        @pl.when(y != yy)
        def _():
            copy(ssend.at[yy], srecv.at[yy], S_Y + (y - yy + 4) % 4, YP).wait_recv()

        for zz in range(4):
            upd[yy, zz] = (latc[yy, zz].astype(F32) + srecv[yy, zz].astype(F32)).astype(BF16)
        cp = copy(upd.at[yy], out.at[yy], OUT + yy, NX)
        cp.start()
        outs.append(cp)

    for cp in sent:
        cp.wait_send()

    def drain(k, _):
        for base in (A_YP, A_YM, A_FP, A_FM):
            a_copy(k, base).wait_send()
        return 0

    lax.fori_loop(0, 8, drain, 0)

    def drain4(k, _):
        p_copy(k).wait_send()

        @pl.when(k != y)
        def _():
            s_copy(k).wait_send()

        return 0

    lax.fori_loop(0, 4, drain4, 0)

    @pl.when(jnp.logical_not(gather))
    def _():
        o_first().wait_send()

    @pl.when(gather)
    def _():
        o_copy("o_xh", XH).wait_send()

    @pl.when(active)
    def _():
        for name, dev in (("o_zp", ZP), ("o_zm", ZM), ("o_fp", ZP), ("o_fm", ZM), ("o_co0", CO), ("o_co1", CO), ("o_co2", CO), ("o_co3", CO)):
            o_copy(name, dev).wait_send()

    for cp in outs:
        cp.wait()


def body(latents, gain, mod_table, slot_noise_level, key_block_index, counts, w_qkv, w_out):
    vmem = pl.BlockSpec(memory_space=pltpu.VMEM)
    smem = pl.BlockSpec(memory_space=pltpu.SMEM)
    hbm = pl.BlockSpec(memory_space=pl.ANY)
    blocks = (4, 4, ROWS, PIECE)
    out = pl.pallas_call(
        kernel,
        out_shape=jax.ShapeDtypeStruct(blocks, BF16),
        in_specs=[vmem, vmem, vmem, smem, smem, smem, hbm, hbm],
        out_specs=hbm,
        scratch_shapes=[
            pltpu.VMEM((8, ROWS, D), BF16),
            pltpu.VMEM((D, QKV), BF16),
            pltpu.VMEM((4, 4 * GROUP, PIECE), BF16),
            pltpu.VMEM((8, ROWS, GROUP), BF16),
            pltpu.VMEM((16, ROWS, 2 * GROUP), BF16),
            pltpu.VMEM((8, ROWS, 4 * GROUP), BF16),
            pltpu.VMEM((2 * ROWS, QKV), F32),
            pltpu.VMEM(blocks, BF16),
            pltpu.VMEM(blocks, BF16),
            pltpu.VMEM(blocks, BF16),
            pltpu.VMEM(blocks, BF16),
            pltpu.VMEM(blocks, BF16),
            pltpu.VMEM(blocks, BF16),
            pltpu.SemaphoreType.DMA((4,)),
            pltpu.SemaphoreType.DMA((N_SEM,)),
            pltpu.SemaphoreType.DMA((N_SEM,)),
        ],
        compiler_params=pltpu.CompilerParams(
            collective_id=0, has_side_effects=True, vmem_limit_bytes=60 * 2**20
        ),
        name="window",
    )(latents[0], gain[None], mod_table, slot_noise_level, key_block_index[0], counts[0], w_qkv, w_out)
    return out.transpose(2, 1, 0, 3).reshape(1, ROWS, D)


def solution(mesh):
    in_specs = (
        P("slot", "tok", None),
        P(),
        P(),
        P("slot"),
        P("slot", None, None),
        P("slot", None),
        P(None, "slot", "tok"),
        P("tok", "slot"),
    )
    out_specs = P("slot", "tok", None)
    return jax.shard_map(body, mesh=mesh, in_specs=in_specs, out_specs=out_specs, check_vma=False)
```

```python
import functools
import math

import jax
import jax.numpy as jnp
from jax import lax
from jax.experimental import pallas as pl
from jax.experimental.pallas import tpu as pltpu
from jax.sharding import PartitionSpec as P

MESH = pl.DeviceIdType.MESH
BF16 = jnp.bfloat16
F32 = jnp.float32

HD = 128
BLK = 128
ROWS = 128
D = 5120
QKV = 1152
PIECE = 320
HALF = 64
NTILE = 256
COLS = 1280
GROUP = 384

NAMES = (
    "w_xh", "w_zp0", "w_zm0", "w_co0", "w_zp1", "w_zm1", "w_co1", "w_fp0", "w_fm0", "w_co2", "w_co3",
    "w_fp1", "w_fm1", "w_co4", "w_co5", "w_co6", "w_co7", "t_x0", "t_x1", "t_yp0", "t_yp1", "t_ym0", "t_ym1",
    "t_fp", "t_fm", "u_yp0", "u_yp1", "u_ym0", "u_ym1", "u_fp", "u_fm", "u_x", "o_a0", "o_a1", "o_a2",
    "o_a3", "o_xh", "o_zp", "o_zm", "o_fp", "o_fm", "o_co0", "o_co1", "o_co2", "o_co3",
)
SEM = {name: i for i, name in enumerate(NAMES)}
KV0 = len(NAMES)
A_YP = KV0 + 8
A_YM = A_YP + 8
A_FP = A_YM + 8
A_FM = A_FP + 8
P_X = A_FM + 8
S_Y = P_X + 4
LAT = S_Y + 4
N_SEM = LAT + 1
ORDER = (3, 1, 2, 0)
SEND_P = (1, 2, 3, 0)
SEND_M = (3, 2, 0, 1)
FORWARD = (2, 3, 0, 1)


def kernel(lat, gain, mod, level, ids, counts, wq, wo, branch, lat_prev,
           x, w, wot, wout, q, ctx, att, psend, precv, ssend, local, ss, rs):
    s, t = lax.axis_index("slot"), lax.axis_index("tok")
    z, h, c = s // 4, (s // 2) % 2, s % 2
    y, l = t // 2, t % 2

    def slot(zz, hh, cc):
        return (zz % 4) * 4 + hh * 2 + cc

    def tok(yy, ll):
        return (yy % 4) * 2 + ll

    XL = (s, tok(y, 1 - l))
    YP, YM, Y2 = (s, tok(y + 1, l)), (s, tok(y + 3, l)), (s, tok(y + 2, l))
    ZP, ZM = (slot(z + 1, h, c), t), (slot(z + 3, h, c), t)
    XH, CO = (slot(z, 1 - h, c), t), (slot(z, h, 1 - c), t)
    NX, PV = ((s + 1) % 16, t), ((s + 15) % 16, t)

    def copy(src, dst, sem, dev):
        k = SEM[sem] if isinstance(sem, str) else sem
        return pltpu.make_async_remote_copy(
            src_ref=src, dst_ref=dst, send_sem=ss.at[k], recv_sem=rs.at[k], device_id=dev, device_id_type=MESH
        )

    sent = []

    def send(ref, sem, dev):
        cp = copy(ref, ref, sem, dev)
        cp.start()
        sent.append(cp)
        return cp

    barrier = pltpu.get_barrier_semaphore()
    here, before = (l + c) % 2, (l + 1 - c) % 2
    peers = [XL, YP, YM, Y2, ZP, ZM, XH, CO, NX, PV]
    peers += [(NX[0], tok(yy, here)) for yy in range(4)] + [(PV[0], tok(yy, before)) for yy in range(4)]
    for dev in peers:
        pl.semaphore_signal(barrier, inc=1, device_id=dev, device_id_type=MESH)

    def wrows(piece, first=0, size=PIECE):
        return w.at[pl.ds(pl.multiple_of(piece * PIECE + first, 32), size)]

    own = [
        pltpu.make_async_copy(
            wq.at[j], w.at[pl.ds(pl.multiple_of(s * PIECE, 64), PIECE), pl.ds(j * GROUP, GROUP)], local.at[j]
        )
        for j in range(3)
    ]
    for cp in own:
        cp.start()
    for cp in own:
        cp.wait()
    pl.semaphore_wait(barrier, len(peers))

    mine = wrows(s)
    w_xh = send(mine, "w_xh", XH)
    w_zp0 = send(mine, "w_zp0", ZP)
    w_zm0 = send(mine, "w_zm0", ZM)
    w_co = [send(mine, "w_co0", CO)]

    lv = level[0]
    factor = gain[...] * (1.0 + mod[lv, 0:1, :])
    offset = mod[lv, 1:2, :]

    def norm(i, _):
        rows = pl.ds(pl.multiple_of(i * 16, 16), 16)
        xf = lat[rows, :].astype(F32)
        mean = jnp.mean(xf, axis=-1, keepdims=True)
        centred = xf - mean
        var = jnp.mean(centred * centred, axis=-1, keepdims=True)
        x[t, rows, :] = (centred * lax.rsqrt(var + 1e-06) * factor + offset).astype(BF16)
        return 0

    def shard(tt, half):
        return x.at[tt, pl.ds(half * HALF, HALF)]

    t_x, t_yp, t_ym = [], [], []
    for half in range(2):
        lax.fori_loop(half * 4, half * 4 + 4, norm, 0)
        t_yp.append(send(shard(t, half), "t_yp%d" % half, YP))
        t_ym.append(send(shard(t, half), "t_ym%d" % half, YM))
        t_x.append(send(shard(t, half), "t_x%d" % half, XL))

    yd = 2 * h + c
    gather = y == yd
    active = c == y % 2
    relay = active & (h != y // 2)

    def ocols(zz):
        return pl.ds(pl.multiple_of((zz % 4) * PIECE, 64), PIECE)

    def lanes(yy):
        return pl.ds(pl.multiple_of((yy % 4) * GROUP, 128), GROUP)

    def o_first():
        return copy(wo, wot.at[ocols(z), lanes(y)], SEM["o_a0"] + (y - yd + 4) % 4, (s, tok(yd, l)))

    def o_copy(name, dev, zz):
        ref = wot.at[ocols(zz)]
        if name == "o_fp":
            ref = wot.at[ocols(zz), pl.ds(0, 768)]
        elif name == "o_fm":
            ref = wot.at[ocols(zz), pl.ds(768, 768)]
        return copy(ref, ref, name, dev)

    @pl.when(jnp.logical_not(gather))
    def _():
        o_first().start()

    @pl.when(gather)
    def _():
        cp = pltpu.make_async_copy(wo, wot.at[ocols(z), lanes(y)], local.at[3])
        cp.start()
        cp.wait()

    tm, tp, tx = tok(y + 3, l), tok(y + 1, l), tok(y, 1 - l)
    t2 = tok(y + 2, l)
    um, up, u2 = tok(y + 3, 1 - l), tok(y + 1, 1 - l), tok(y + 2, 1 - l)

    @pl.when(gather)
    def _():
        for d in range(1, 4):
            src = wot.at[ocols(z), lanes(0)]
            copy(src, src, SEM["o_a0"] + d, YP).wait_recv()
        o_copy("o_xh", XH, z).start()

    t_yp[0].wait_recv()
    t_fp = send(shard(tm, 0), "t_fp", YP)
    w_zp0.wait_recv()
    pm = slot(z + 3, h, c)
    w_fp0 = send(wrows(pm, 0, PIECE // 2), "w_fp0", ZP)
    w_co.append(send(wrows(pm), "w_co2", CO))
    w_zm0.wait_recv()
    pp = slot(z + 1, h, c)
    w_fm0 = send(wrows(pp, PIECE // 2, PIECE // 2), "w_fm0", ZM)
    w_co.append(send(wrows(pp), "w_co3", CO))
    w_xh.wait_recv()
    px = slot(z, 1 - h, c)
    w_zp1 = send(wrows(px), "w_zp1", ZP)
    w_zm1 = send(wrows(px), "w_zm1", ZM)
    w_co.append(send(wrows(px), "w_co1", CO))
    u_yp, u_ym = [], []

    def second(half):
        t_x[half].wait_recv()
        u_yp.append(send(shard(tx, half), "u_yp%d" % half, YP))
        u_ym.append(send(shard(tx, half), "u_ym%d" % half, YM))

    second(0)
    t_ym[1].wait_recv()
    t_fm = send(shard(tp, 1), "t_fm", YM)
    second(1)

    w_zp1.wait_recv()
    pm1 = slot(z + 3, 1 - h, c)
    w_fp1 = send(wrows(pm1, 0, PIECE // 2), "w_fp1", ZP)
    w_co.append(send(wrows(pm1), "w_co4", CO))
    w_zm1.wait_recv()
    pp1 = slot(z + 1, 1 - h, c)
    w_fm1 = send(wrows(pp1, PIECE // 2, PIECE // 2), "w_fm1", ZM)
    w_co.append(send(wrows(pp1), "w_co5", CO))

    @pl.when(relay)
    def _():
        o_copy("o_xh", XH, z).wait_recv()

    @pl.when(active)
    def _():
        o_copy("o_zp", ZP, z).start()
        o_copy("o_zm", ZM, z).start()
        o_copy("o_co0", CO, z).start()

    w_fp0.wait_recv()
    w_fm0.wait_recv()
    w_co.append(send(wrows(slot(z + 2, h, c)), "w_co6", CO))
    t_fm.wait_recv()
    u_x = send(shard(t2, 1), "u_x", XL)

    w_fp1.wait_recv()
    w_fm1.wait_recv()
    w_co.append(send(wrows(slot(z + 2, 1 - h, c)), "w_co7", CO))
    for cp in w_co:
        cp.wait_recv()

    def quarter(tt, part):
        return x.at[tt, pl.ds(part * 32, 32)]

    def u_forward():
        a, b = quarter(um, 0), quarter(up, 1)
        return copy(a, a, "u_fp", YP), copy(b, b, "u_fm", YM)

    def kv_copy(tt, k):
        return copy(ctx.at[tt], ctx.at[8 + tt], KV0 + k, NX)

    def project(b, _):
        @pl.when(b == 1)
        def _():
            t_yp[1].wait_recv()
            t_ym[0].wait_recv()

        @pl.when(b == 2)
        def _():
            u_yp[1].wait_recv()
            u_ym[1].wait_recv()

        @pl.when(b == 3)
        def _():
            t_fp.wait_recv()
            u_x.wait_recv()
            for cp in u_forward():
                cp.wait_recv()

        def pick(values):
            return jnp.where(b == 0, values[0], jnp.where(b == 1, values[1], jnp.where(b == 2, values[2], values[3])))

        ta, tb = pick((t, tm, um, t2)), pick((tx, tp, up, u2))
        rows = jnp.concatenate([x[ta], x[tb]], axis=0)
        for n in range(3):
            cols = slice(n * NTILE, (n + 1) * NTILE)
            part = jnp.dot(rows, w[:, GROUP + n * NTILE:GROUP + (n + 1) * NTILE], preferred_element_type=F32).astype(BF16)
            ctx[ta, :, cols] = part[:ROWS]
            ctx[tb, :, cols] = part[ROWS:]
        kv_copy(ta, 2 * b).start()
        kv_copy(tb, 2 * b + 1).start()
        part = jnp.dot(rows, w[:, :GROUP], preferred_element_type=F32).astype(BF16)
        q[ta] = part[:ROWS]
        q[tb] = part[ROWS:]
        return 0

    u_yp[0].wait_recv()
    u_ym[0].wait_recv()
    for cp in u_forward():
        cp.start()
    lax.fori_loop(0, 4, project, 0)
    lat_copy = copy(lat, lat_prev, LAT, NX)
    lat_copy.start()

    @pl.when(active)
    def _():
        o_copy("o_zp", ZP, z + 3).wait_recv()
        o_copy("o_fp", ZP, z + 3).start()
        o_copy("o_co1", CO, z + 3).start()
        o_copy("o_zm", ZM, z + 1).wait_recv()
        o_copy("o_fm", ZM, z + 1).start()
        o_copy("o_co2", CO, z + 1).start()

    for k in range(8):
        kv_copy(t, k).wait_recv()

    scale = 1.0 / math.sqrt(HD)

    def owner(j):
        return (y + 1 + j) % 4

    def tile_at(yt, second_half):
        return 2 * (yt % 4) + jnp.where(second_half, here, 1 - here)

    def a_copy(j, late, base):
        if base == A_YP:
            ref, dev = att.at[tile_at(y + 1 + j, late), :, lanes(y)], YP
        elif base == A_YM:
            ref, dev = att.at[tile_at(y + 1 + j, late), :, lanes(y)], YM
        elif base == A_FP:
            ref, dev = att.at[tile_at(y + j, late), pl.ds(0, HALF), lanes(y + 3)], YP
        else:
            ref, dev = att.at[tile_at(y + 2 + j, late), pl.ds(HALF, HALF), lanes(y + 1)], YM
        return copy(ref, ref, base + j + jnp.where(late, 4, 0), dev)

    def at(k, values):
        return jnp.where(k == 0, values[0], jnp.where(k == 1, values[1], jnp.where(k == 2, values[2], values[3])))

    def attend(i):
        listed = [ids[j, i] for j in range(4)]
        valid = []
        for j in range(4):
            ok = j < counts[i]
            for e in range(j):
                ok = ok & (listed[e] != listed[j])
            valid.append(ok)
        outs = []
        for head in range(3):
            hc = slice(head * HD, (head + 1) * HD)
            vc = slice(GROUP + head * HD, GROUP + (head + 1) * HD)
            keys = jnp.concatenate([ctx[listed[j], :, hc] for j in range(4)], axis=0)
            scores = lax.dot_general(q[i, :, hc], keys, (((1,), (1,)), ((), ())), preferred_element_type=F32) * scale
            scores = [jnp.where(valid[j], scores[:, j * BLK:(j + 1) * BLK], -1e30) for j in range(4)]
            top = jnp.maximum(jnp.maximum(scores[0], scores[1]), jnp.maximum(scores[2], scores[3]))
            top = jnp.max(top, axis=1, keepdims=True)
            expo = [jnp.exp(sc - top) for sc in scores]
            total = jnp.sum((expo[0] + expo[1]) + (expo[2] + expo[3]), axis=1, keepdims=True)
            probs = jnp.concatenate([(e / total).astype(BF16) for e in expo], axis=1)
            values = jnp.concatenate([ctx[listed[j], :, vc] for j in range(4)], axis=0)
            outs.append(jnp.dot(probs, values, preferred_element_type=F32).astype(BF16))
        att[i, :, lanes(y)] = jnp.concatenate(outs, axis=1)

    def forward(k, late):
        j = at(k, FORWARD)
        a_copy(j, late, A_YP).wait_recv()
        a_copy(j, late, A_FP).start()
        a_copy(j, late, A_YM).wait_recv()
        a_copy(j, late, A_FM).start()

    def attention(k, _):
        late = k >= 4
        j = at(k % 4, ORDER)
        attend(tile_at(y + 1 + j, late))

        @pl.when(k == 0)
        def _():
            a_copy(3, False, A_YM).start()

        @pl.when(k == 1)
        def _():
            a_copy(1, False, A_YP).start()

        @pl.when(k == 2)
        def _():
            a_copy(2, False, A_YP).start()
            a_copy(2, False, A_YM).start()

        @pl.when(k == 3)
        def _():
            a_copy(0, False, A_YM).start()
            a_copy(3, False, A_YP).start()
            a_copy(1, False, A_YM).start()
            a_copy(0, False, A_YP).start()

        @pl.when(late)
        def _():
            a_copy(j, True, A_YP).start()
            a_copy(j, True, A_YM).start()
            forward(k - 4, False)

        return 0

    lax.fori_loop(0, 8, attention, 0)

    CORE = ("o_co0", "o_co1", "o_co2", "o_co3")

    @pl.when(active)
    def _():
        o_copy("o_fp", ZP, z + 2).wait_recv()
        o_copy("o_fm", ZM, z + 2).wait_recv()
        o_copy("o_co3", CO, z + 2).start()

    @pl.when(jnp.logical_not(active))
    def _():
        for name in CORE:
            o_copy(name, CO, z).wait_recv()

    def turn(r, _):
        rows = pl.ds(pl.multiple_of(r * 128, 128), 128)
        wout[:, rows] = wot[rows, :].T
        return 0

    lax.fori_loop(0, 10, turn, 0)

    def product(p, late):
        j = (p + 2) % 4
        a_copy(j, late, A_FP).wait_recv()
        a_copy(j, late, A_FM).wait_recv()
        return jnp.dot(att[tile_at(y + 1 + p, late)], wout[...], preferred_element_type=F32)

    def p_copy(p):
        return copy(psend.at[p], precv.at[p], P_X + p, XL)

    def foreign(p, _):
        psend[p] = product(p, False).astype(BF16)
        p_copy(p).start()
        forward(p, True)
        return 0

    lax.fori_loop(0, 4, foreign, 0)

    def s_copy(p):
        return copy(ssend.at[p], branch.at[y], S_Y + p, (NX[0], tok(y + 1 + p, here)))

    def finish(p, _):
        mine = product(p, True)
        p_copy(p).wait_recv()
        ssend[p] = (mine + precv[p].astype(F32)).astype(BF16)
        s_copy(p).start()
        return 0

    lax.fori_loop(0, 4, finish, 0)

    for cp in sent:
        cp.wait_send()
    for cp in u_forward():
        cp.wait_send()

    def drain(k, _):
        kv_copy(t, k).wait_send()
        for base in (A_YP, A_YM, A_FP, A_FM):
            a_copy(k % 4, k >= 4, base).wait_send()
        return 0

    lax.fori_loop(0, 8, drain, 0)
    for p in range(4):
        p_copy(p).wait_send()
        s_copy(p).wait_send()
    lat_copy.wait_send()

    @pl.when(jnp.logical_not(gather))
    def _():
        o_first().wait_send()

    @pl.when(gather)
    def _():
        o_copy("o_xh", XH, z).wait_send()

    @pl.when(active)
    def _():
        for name in ("o_zp", "o_zm", "o_fp", "o_fm") + CORE:
            o_copy(name, CO, z).wait_send()

    lat_copy.wait_recv()
    for p in range(4):
        s_copy(p).wait_recv()


def residual(branch, lat, out):
    for zz in range(4):
        cols = slice(zz * COLS, (zz + 1) * COLS)
        pieces = [branch[yy, :, zz * PIECE:(zz + 1) * PIECE].astype(F32) for yy in range(4)]
        out[:, cols] = (lat[:, cols].astype(F32) + jnp.concatenate(pieces, axis=1)).astype(BF16)


def body(latents, gain, mod_table, slot_noise_level, key_block_index, counts, w_qkv, w_out):
    vmem = pl.BlockSpec(memory_space=pltpu.VMEM)
    smem = pl.BlockSpec(memory_space=pltpu.SMEM)
    hbm = pl.BlockSpec(memory_space=pl.ANY)
    blocks = pltpu.VMEM((4, ROWS, COLS), BF16)
    branch, lat_prev = pl.pallas_call(
        kernel,
        out_shape=[jax.ShapeDtypeStruct((4, ROWS, COLS), BF16), jax.ShapeDtypeStruct((ROWS, D), BF16)],
        in_specs=[vmem, vmem, vmem, smem, smem, smem, hbm, hbm],
        out_specs=[hbm, hbm],
        scratch_shapes=[
            pltpu.VMEM((8, ROWS, D), BF16),
            pltpu.VMEM((D, QKV), BF16),
            pltpu.VMEM((COLS, 4 * GROUP), BF16),
            pltpu.VMEM((4 * GROUP, COLS), BF16),
            pltpu.VMEM((8, ROWS, GROUP), BF16),
            pltpu.VMEM((16, ROWS, 2 * GROUP), BF16),
            pltpu.VMEM((8, ROWS, 4 * GROUP), BF16),
            blocks,
            blocks,
            blocks,
            pltpu.SemaphoreType.DMA((4,)),
            pltpu.SemaphoreType.DMA((N_SEM,)),
            pltpu.SemaphoreType.DMA((N_SEM,)),
        ],
        compiler_params=pltpu.CompilerParams(
            collective_id=0, has_side_effects=True, vmem_limit_bytes=60 * 2**20
        ),
        name="window",
    )(latents[0], gain[None], mod_table, slot_noise_level, key_block_index[0].T, counts[0], w_qkv, w_out.T)
    out = pl.pallas_call(
        residual,
        grid=(4,),
        out_shape=jax.ShapeDtypeStruct((ROWS, D), BF16),
        in_specs=[pl.BlockSpec((4, ROWS // 4, COLS), lambda i: (0, i, 0)), pl.BlockSpec((ROWS // 4, D), lambda i: (i, 0))],
        out_specs=pl.BlockSpec((ROWS // 4, D), lambda i: (i, 0)),
        name="residual",
    )(branch, lat_prev)
    return out[None]


def solution(mesh):
    in_specs = (
        P("slot", "tok", None),
        P(),
        P(),
        P("slot"),
        P("slot", None, None),
        P("slot", None),
        P(None, "slot", "tok"),
        P("tok", "slot"),
    )
    out_specs = P("slot", "tok", None)
    return jax.shard_map(body, mesh=mesh, in_specs=in_specs, out_specs=out_specs, check_vma=False)
```

```python
import functools
import math

import jax
import jax.numpy as jnp
from jax import lax
from jax.experimental import pallas as pl
from jax.experimental.pallas import tpu as pltpu
from jax.sharding import PartitionSpec as P

MESH = pl.DeviceIdType.MESH
BF16 = jnp.bfloat16
F32 = jnp.float32

HD = 128
BLK = 128
ROWS = 128
D = 5120
QKV = 1152
PIECE = 320
HALF = 64
NTILE = 256
COLS = 1280
GROUP = 384

NAMES = (
    "w_xh", "w_zp0", "w_zm0", "w_co0", "w_zp1", "w_zm1", "w_co1", "w_fp0", "w_fm0", "w_co2", "w_co3",
    "w_fp1", "w_fm1", "w_co4", "w_co5", "w_co6", "w_co7", "t_x0", "t_x1", "t_yp0", "t_yp1", "t_ym0", "t_ym1",
    "t_fp", "t_fm", "u_yp0", "u_yp1", "u_ym0", "u_ym1", "u_fp", "u_fm", "u_x", "o_a0", "o_a1", "o_a2",
    "o_a3", "o_xh", "o_zp", "o_zm", "o_z2", "o_co0", "o_co1", "o_co2", "o_co3",
)
SEM = {name: i for i, name in enumerate(NAMES)}
KV0 = len(NAMES)
A_YP = KV0 + 16
A_YM = A_YP + 8
A_FP = A_YM + 8
A_FM = A_FP + 8
P_X = A_FM + 8
S_Y = P_X + 4
LAT = S_Y + 4
N_SEM = LAT + 1
ORDER = (3, 1, 2, 0)
SEND_P = (1, 2, 3, 0)
SEND_M = (3, 2, 0, 1)
FORWARD = (2, 3, 0, 1)


def kernel(lat, gain, mod, level, ids, counts, wq, wo, branch, lat_prev,
           x, w, wot, wout, q, ctx, att, psend, precv, ssend, local, ss, rs):
    s, t = lax.axis_index("slot"), lax.axis_index("tok")
    z, h, c = s // 4, (s // 2) % 2, s % 2
    y, l = t // 2, t % 2

    def slot(zz, hh, cc):
        return (zz % 4) * 4 + hh * 2 + cc

    def tok(yy, ll):
        return (yy % 4) * 2 + ll

    XL = (s, tok(y, 1 - l))
    YP, YM, Y2 = (s, tok(y + 1, l)), (s, tok(y + 3, l)), (s, tok(y + 2, l))
    ZP, ZM = (slot(z + 1, h, c), t), (slot(z + 3, h, c), t)
    XH, CO = (slot(z, 1 - h, c), t), (slot(z, h, 1 - c), t)
    NX, PV = ((s + 1) % 16, t), ((s + 15) % 16, t)

    def copy(src, dst, sem, dev):
        k = SEM[sem] if isinstance(sem, str) else sem
        return pltpu.make_async_remote_copy(
            src_ref=src, dst_ref=dst, send_sem=ss.at[k], recv_sem=rs.at[k], device_id=dev, device_id_type=MESH
        )

    sent = []

    def send(ref, sem, dev):
        cp = copy(ref, ref, sem, dev)
        cp.start()
        sent.append(cp)
        return cp

    barrier = pltpu.get_barrier_semaphore()
    here, before = (l + c) % 2, (l + 1 - c) % 2
    peers = [XL, YP, YM, Y2, ZP, ZM, XH, CO, NX, PV]
    peers += [(NX[0], tok(yy, here)) for yy in range(4)] + [(PV[0], tok(yy, before)) for yy in range(4)]
    for dev in peers:
        pl.semaphore_signal(barrier, inc=1, device_id=dev, device_id_type=MESH)

    def wrows(piece, first=0, size=PIECE):
        return w.at[pl.ds(pl.multiple_of(piece * PIECE + first, 32), size)]

    own = [
        pltpu.make_async_copy(
            wq.at[j], w.at[pl.ds(pl.multiple_of(s * PIECE, 64), PIECE), pl.ds(j * GROUP, GROUP)], local.at[j]
        )
        for j in range(3)
    ]
    for cp in own:
        cp.start()
    lv = level[0]
    factor = gain[...] * (1.0 + mod[lv, 0:1, :])
    offset = mod[lv, 1:2, :]

    def norm(i, _):
        rows = pl.ds(pl.multiple_of(i * 16, 16), 16)
        xf = lat[rows, :].astype(F32)
        mean = jnp.mean(xf, axis=-1, keepdims=True)
        centred = xf - mean
        var = jnp.mean(centred * centred, axis=-1, keepdims=True)
        x[t, rows, :] = (centred * lax.rsqrt(var + 1e-06) * factor + offset).astype(BF16)
        return 0

    lax.fori_loop(0, 4, norm, 0)
    for cp in own:
        cp.wait()
    pl.semaphore_wait(barrier, len(peers))

    yd = 2 * h + c
    gather = y == yd
    active = c == y % 2
    relay = active & (h != y // 2)

    def ocols(zz):
        return pl.ds(pl.multiple_of((zz % 4) * PIECE, 64), PIECE)

    def lanes(yy):
        return pl.ds(pl.multiple_of((yy % 4) * GROUP, 128), GROUP)

    def o_first():
        return copy(wo, wot.at[ocols(z), lanes(y)], SEM["o_a0"] + (y - yd + 4) % 4, (s, tok(yd, l)))

    def o_copy(name, dev, zz):
        ref = wot.at[ocols(zz)]
        return copy(ref, ref, name, dev)

    @pl.when(jnp.logical_not(gather))
    def _():
        o_first().start()

    @pl.when(gather)
    def _():
        cp = pltpu.make_async_copy(wo, wot.at[ocols(z), lanes(y)], local.at[3])
        cp.start()
        cp.wait()

    mine = wrows(s)
    w_xh = send(mine, "w_xh", XH)
    w_zp0 = send(mine, "w_zp0", ZP)
    w_zm0 = send(mine, "w_zm0", ZM)
    w_co = [send(mine, "w_co0", CO)]

    def shard(tt, half):
        return x.at[tt, pl.ds(half * HALF, HALF)]

    t_x, t_yp, t_ym = [], [], []
    for half in range(2):
        if half == 1:
            lax.fori_loop(4, 8, norm, 0)
        t_yp.append(send(shard(t, half), "t_yp%d" % half, YP))
        t_ym.append(send(shard(t, half), "t_ym%d" % half, YM))
        t_x.append(send(shard(t, half), "t_x%d" % half, XL))

    tm, tp, tx = tok(y + 3, l), tok(y + 1, l), tok(y, 1 - l)
    t2 = tok(y + 2, l)
    um, up, u2 = tok(y + 3, 1 - l), tok(y + 1, 1 - l), tok(y + 2, 1 - l)

    @pl.when(gather)
    def _():
        for d in range(1, 4):
            src = wot.at[ocols(z), lanes(0)]
            copy(src, src, SEM["o_a0"] + d, YP).wait_recv()
        o_copy("o_xh", XH, z).start()

    t_yp[0].wait_recv()
    t_fp = send(shard(tm, 0), "t_fp", YP)
    w_zp0.wait_recv()
    pm = slot(z + 3, h, c)
    w_fp0 = send(wrows(pm, 0, PIECE // 2), "w_fp0", ZP)
    w_co.append(send(wrows(pm), "w_co2", CO))
    w_zm0.wait_recv()
    pp = slot(z + 1, h, c)
    w_fm0 = send(wrows(pp, PIECE // 2, PIECE // 2), "w_fm0", ZM)
    w_co.append(send(wrows(pp), "w_co3", CO))
    w_xh.wait_recv()
    px = slot(z, 1 - h, c)
    w_zp1 = send(wrows(px), "w_zp1", ZP)
    w_zm1 = send(wrows(px), "w_zm1", ZM)
    w_co.append(send(wrows(px), "w_co1", CO))
    u_yp, u_ym = [], []

    def second(half):
        t_x[half].wait_recv()
        u_yp.append(send(shard(tx, half), "u_yp%d" % half, YP))
        u_ym.append(send(shard(tx, half), "u_ym%d" % half, YM))

    second(0)
    t_ym[1].wait_recv()
    t_fm = send(shard(tp, 1), "t_fm", YM)
    second(1)

    w_zp1.wait_recv()
    pm1 = slot(z + 3, 1 - h, c)
    w_fp1 = send(wrows(pm1, 0, PIECE // 2), "w_fp1", ZP)
    w_co.append(send(wrows(pm1), "w_co4", CO))
    w_zm1.wait_recv()
    pp1 = slot(z + 1, 1 - h, c)
    w_fm1 = send(wrows(pp1, PIECE // 2, PIECE // 2), "w_fm1", ZM)
    w_co.append(send(wrows(pp1), "w_co5", CO))

    def spread():
        for name, dev in (("o_zp", ZP), ("o_zm", ZM), ("o_co0", CO)):
            o_copy(name, dev, z).start()

    @pl.when(relay)
    def _():
        o_copy("o_xh", XH, z).wait_recv()

    @pl.when(active)
    def _():
        spread()

    w_fp0.wait_recv()
    w_fm0.wait_recv()
    w_co.append(send(wrows(slot(z + 2, h, c)), "w_co6", CO))
    t_fm.wait_recv()
    u_x = send(shard(t2, 1), "u_x", XL)

    w_fp1.wait_recv()
    w_fm1.wait_recv()
    w_co.append(send(wrows(slot(z + 2, 1 - h, c)), "w_co7", CO))
    for cp in w_co:
        cp.wait_recv()

    def quarter(tt, part):
        return x.at[tt, pl.ds(part * 32, 32)]

    def u_forward():
        a, b = quarter(um, 0), quarter(up, 1)
        return copy(a, a, "u_fp", YP), copy(b, b, "u_fm", YM)

    def kv_copy(tt, half, k):
        rows = pl.ds(pl.multiple_of(half * HALF, HALF), HALF)
        return copy(ctx.at[tt, rows], ctx.at[8 + tt, rows], KV0 + k, NX)

    def project(b, _):
        @pl.when(b == 1)
        def _():
            @pl.when(active)
            def _():
                o_copy("o_zm", ZM, z + 1).wait_recv()
                o_copy("o_z2", ZM, z + 1).start()

            t_yp[1].wait_recv()
            t_ym[0].wait_recv()

        @pl.when(b == 2)
        def _():
            t_fp.wait_recv()

        @pl.when(b == 3)
        def _():
            u_yp[1].wait_recv()
            u_ym[1].wait_recv()
            u_x.wait_recv()
            for cp in u_forward():
                cp.wait_recv()

        def pick(values):
            return jnp.where(b == 0, values[0], jnp.where(b == 1, values[1], jnp.where(b == 2, values[2], values[3])))

        first = pick((0, 0, 0, 1))
        parts = (
            (pick((t, tm, um, um)), first),
            (pick((t, tm, up, up)), pick((1, 1, 0, 1))),
            (pick((tx, tp, t2, u2)), 0),
            (pick((tx, tp, t2, u2)), 1),
        )
        parts = [(tt, half, pl.ds(pl.multiple_of(half * HALF, HALF), HALF)) for tt, half in parts]
        rows = jnp.concatenate([x[tt, rr, :] for tt, half, rr in parts], axis=0)
        for n in range(3):
            cols = slice(n * NTILE, (n + 1) * NTILE)
            part = jnp.dot(rows, w[:, GROUP + n * NTILE:GROUP + (n + 1) * NTILE], preferred_element_type=F32).astype(BF16)
            for i, (tt, half, rr) in enumerate(parts):
                ctx[tt, rr, cols] = part[i * HALF:(i + 1) * HALF]
        for i, (tt, half, rr) in enumerate(parts):
            kv_copy(tt, half, 4 * b + i).start()
        part = jnp.dot(rows, w[:, :GROUP], preferred_element_type=F32).astype(BF16)
        for i, (tt, half, rr) in enumerate(parts):
            q[tt, rr, :] = part[i * HALF:(i + 1) * HALF]
        return 0

    u_yp[0].wait_recv()
    u_ym[0].wait_recv()
    for cp in u_forward():
        cp.start()
    lax.fori_loop(0, 4, project, 0)

    lat_copy = copy(lat, lat_prev, LAT, NX)
    lat_copy.start()

    for k in range(16):
        kv_copy(t, 0, k).wait_recv()

    @pl.when(active)
    def _():
        for name, dz, onward in (("o_zp", 3, "o_co1"), ("o_zm", 1, "o_co2"), ("o_z2", 2, "o_co3")):
            if name != "o_zm":
                o_copy(name, ZP, z + dz).wait_recv()
            o_copy(onward, CO, z + dz).start()

    scale = 1.0 / math.sqrt(HD)

    def owner(j):
        return (y + 1 + j) % 4

    def tile_at(yt, second_half):
        return 2 * (yt % 4) + jnp.where(second_half, here, 1 - here)

    def a_copy(j, late, base):
        if base == A_YP:
            ref, dev = att.at[tile_at(y + 1 + j, late), :, lanes(y)], YP
        elif base == A_YM:
            ref, dev = att.at[tile_at(y + 1 + j, late), :, lanes(y)], YM
        elif base == A_FP:
            ref, dev = att.at[tile_at(y + j, late), pl.ds(0, HALF), lanes(y + 3)], YP
        else:
            ref, dev = att.at[tile_at(y + 2 + j, late), pl.ds(HALF, HALF), lanes(y + 1)], YM
        return copy(ref, ref, base + j + jnp.where(late, 4, 0), dev)

    def at(k, values):
        return jnp.where(k == 0, values[0], jnp.where(k == 1, values[1], jnp.where(k == 2, values[2], values[3])))

    def attend(i):
        listed = [ids[j, i] for j in range(4)]
        valid = []
        for j in range(4):
            ok = j < counts[i]
            for e in range(j):
                ok = ok & (listed[e] != listed[j])
            valid.append(ok)
        outs = []
        for head in range(3):
            hc = slice(head * HD, (head + 1) * HD)
            vc = slice(GROUP + head * HD, GROUP + (head + 1) * HD)
            keys = jnp.concatenate([ctx[listed[j], :, hc] for j in range(4)], axis=0)
            scores = lax.dot_general(q[i, :, hc], keys, (((1,), (1,)), ((), ())), preferred_element_type=F32) * scale
            scores = [jnp.where(valid[j], scores[:, j * BLK:(j + 1) * BLK], -1e30) for j in range(4)]
            top = jnp.maximum(jnp.maximum(scores[0], scores[1]), jnp.maximum(scores[2], scores[3]))
            top = jnp.max(top, axis=1, keepdims=True)
            expo = [jnp.exp(sc - top) for sc in scores]
            total = jnp.sum((expo[0] + expo[1]) + (expo[2] + expo[3]), axis=1, keepdims=True)
            probs = jnp.concatenate([(e / total).astype(BF16) for e in expo], axis=1)
            values = jnp.concatenate([ctx[listed[j], :, vc] for j in range(4)], axis=0)
            outs.append(jnp.dot(probs, values, preferred_element_type=F32).astype(BF16))
        att[i, :, lanes(y)] = jnp.concatenate(outs, axis=1)

    def forward(k, late):
        j = at(k, FORWARD)
        a_copy(j, late, A_YP).wait_recv()
        a_copy(j, late, A_FP).start()
        a_copy(j, late, A_YM).wait_recv()
        a_copy(j, late, A_FM).start()

    def attention(k, _):
        late = k >= 4
        j = at(k % 4, ORDER)
        attend(tile_at(y + 1 + j, late))

        @pl.when(k == 0)
        def _():
            a_copy(3, False, A_YM).start()

        @pl.when(k == 1)
        def _():
            a_copy(1, False, A_YP).start()

        @pl.when(k == 2)
        def _():
            a_copy(2, False, A_YP).start()
            a_copy(2, False, A_YM).start()

        @pl.when(k == 3)
        def _():
            a_copy(0, False, A_YM).start()
            a_copy(3, False, A_YP).start()
            a_copy(1, False, A_YM).start()
            a_copy(0, False, A_YP).start()

        @pl.when(late)
        def _():
            a_copy(j, True, A_YP).start()
            a_copy(j, True, A_YM).start()
            forward(k - 4, False)

        return 0

    lax.fori_loop(0, 8, attention, 0)

    CORE = ("o_co0", "o_co1", "o_co2", "o_co3")

    @pl.when(jnp.logical_not(active))
    def _():
        for name in CORE:
            o_copy(name, CO, z).wait_recv()

    def turn(r, _):
        rows = pl.ds(pl.multiple_of(r * 128, 128), 128)
        wout[:, rows] = wot[rows, :].T
        return 0

    lax.fori_loop(0, 10, turn, 0)

    def product(p, late):
        j = (p + 2) % 4
        a_copy(j, late, A_FP).wait_recv()
        a_copy(j, late, A_FM).wait_recv()
        return jnp.dot(att[tile_at(y + 1 + p, late)], wout[...], preferred_element_type=F32)

    def p_copy(p):
        return copy(psend.at[p], precv.at[p], P_X + p, XL)

    def foreign(p, _):
        psend[p] = product(p, False).astype(BF16)
        p_copy(p).start()
        forward(p, True)
        return 0

    lax.fori_loop(0, 4, foreign, 0)

    def s_copy(p):
        return copy(ssend.at[p], branch.at[y], S_Y + p, (NX[0], tok(y + 1 + p, here)))

    def finish(p, _):
        mine = product(p, True)
        p_copy(p).wait_recv()
        ssend[p] = (mine + precv[p].astype(F32)).astype(BF16)
        s_copy(p).start()
        return 0

    lax.fori_loop(0, 4, finish, 0)

    for cp in sent:
        cp.wait_send()
    for cp in u_forward():
        cp.wait_send()

    def drain(k, _):
        kv_copy(t, 0, 2 * k).wait_send()
        kv_copy(t, 0, 2 * k + 1).wait_send()
        for base in (A_YP, A_YM, A_FP, A_FM):
            a_copy(k % 4, k >= 4, base).wait_send()
        return 0

    lax.fori_loop(0, 8, drain, 0)
    for p in range(4):
        p_copy(p).wait_send()
        s_copy(p).wait_send()
    lat_copy.wait_send()

    @pl.when(jnp.logical_not(gather))
    def _():
        o_first().wait_send()

    @pl.when(gather)
    def _():
        o_copy("o_xh", XH, z).wait_send()

    @pl.when(active)
    def _():
        for name in ("o_zp", "o_zm", "o_z2") + CORE:
            o_copy(name, CO, z).wait_send()

    lat_copy.wait_recv()
    for p in range(4):
        s_copy(p).wait_recv()


def residual(branch, lat, out):
    for zz in range(4):
        cols = slice(zz * COLS, (zz + 1) * COLS)
        pieces = [branch[yy, :, zz * PIECE:(zz + 1) * PIECE] for yy in range(4)]
        out[:, cols] = (lat[:, cols].astype(F32) + jnp.concatenate(pieces, axis=1).astype(F32)).astype(BF16)


def body(latents, gain, mod_table, slot_noise_level, key_block_index, counts, w_qkv, w_out):
    vmem = pl.BlockSpec(memory_space=pltpu.VMEM)
    smem = pl.BlockSpec(memory_space=pltpu.SMEM)
    hbm = pl.BlockSpec(memory_space=pl.ANY)
    blocks = pltpu.VMEM((4, ROWS, COLS), BF16)
    branch, lat_prev = pl.pallas_call(
        kernel,
        out_shape=[jax.ShapeDtypeStruct((4, ROWS, COLS), BF16), jax.ShapeDtypeStruct((ROWS, D), BF16)],
        in_specs=[vmem, vmem, vmem, smem, smem, smem, hbm, hbm],
        out_specs=[hbm, hbm],
        scratch_shapes=[
            pltpu.VMEM((8, ROWS, D), BF16),
            pltpu.VMEM((D, QKV), BF16),
            pltpu.VMEM((COLS, 4 * GROUP), BF16),
            pltpu.VMEM((4 * GROUP, COLS), BF16),
            pltpu.VMEM((8, ROWS, GROUP), BF16),
            pltpu.VMEM((16, ROWS, 2 * GROUP), BF16),
            pltpu.VMEM((8, ROWS, 4 * GROUP), BF16),
            blocks,
            blocks,
            blocks,
            pltpu.SemaphoreType.DMA((4,)),
            pltpu.SemaphoreType.DMA((N_SEM,)),
            pltpu.SemaphoreType.DMA((N_SEM,)),
        ],
        compiler_params=pltpu.CompilerParams(
            collective_id=0, has_side_effects=True, vmem_limit_bytes=60 * 2**20
        ),
        name="window",
    )(latents[0], gain[None], mod_table, slot_noise_level, key_block_index[0].T, counts[0], w_qkv, w_out.T)
    out = pl.pallas_call(
        residual,
        grid=(2,),
        out_shape=jax.ShapeDtypeStruct((ROWS, D), BF16),
        in_specs=[pl.BlockSpec((4, ROWS // 2, COLS), lambda i: (0, i, 0)), pl.BlockSpec((ROWS // 2, D), lambda i: (i, 0))],
        out_specs=pl.BlockSpec((ROWS // 2, D), lambda i: (i, 0)),
        name="residual",
    )(branch, lat_prev)
    return out[None]


def solution(mesh):
    in_specs = (
        P("slot", "tok", None),
        P(),
        P(),
        P("slot"),
        P("slot", None, None),
        P("slot", None),
        P(None, "slot", "tok"),
        P("tok", "slot"),
    )
    out_specs = P("slot", "tok", None)
    return jax.shard_map(body, mesh=mesh, in_specs=in_specs, out_specs=out_specs, check_vma=False)
```

```python
import functools
import math

import jax
import jax.numpy as jnp
from jax import lax
from jax.experimental import pallas as pl
from jax.experimental.pallas import tpu as pltpu
from jax.sharding import PartitionSpec as P

MESH = pl.DeviceIdType.MESH
BF16 = jnp.bfloat16
F32 = jnp.float32

HD = 128
BLK = 128
ROWS = 128
D = 5120
QKV = 1152
PIECE = 320
HALF = 64
NTILE = 256
COLS = 1280
GROUP = 384

NAMES = (
    "w_xh", "w_zp0", "w_zm0", "w_co0", "w_zp1", "w_zm1", "w_co1", "w_fp0", "w_fm0", "w_co2", "w_co3",
    "w_fp1", "w_fm1", "w_co4", "w_co5", "w_co6", "w_co7", "t_x0", "t_x1", "t_yp0", "t_yp1", "t_ym0", "t_ym1",
    "t_fp", "t_fm", "u_yp0", "u_yp1", "u_ym0", "u_ym1", "u_fp", "u_fm", "u_x", "o_a0", "o_a1", "o_a2",
    "o_a3", "o_xh", "o_zp", "o_zm", "o_z2", "o_co0", "o_co1", "o_co2", "o_co3",
)
SEM = {name: i for i, name in enumerate(NAMES)}
KV0 = len(NAMES)
A_YP = KV0 + 16
A_YM = A_YP + 8
A_FP = A_YM + 8
A_FM = A_FP + 8
P_X = A_FM + 8
S_Y = P_X + 4
LAT = S_Y + 4
LAT_Y = LAT + 1
N_SEM = LAT_Y + 4
ORDER = (2, 1, 3, 0)


def kernel(lat, gain, mod, level, ids, counts, wq, wo, branch, lat_prev,
           x, w, wot, wout, q, ctx, att, psend, precv, ssend, latc, latr, local, ss, rs):
    s, t = lax.axis_index("slot"), lax.axis_index("tok")
    z, h, c = s // 4, (s // 2) % 2, s % 2
    y, l = t // 2, t % 2

    def slot(zz, hh, cc):
        return (zz % 4) * 4 + hh * 2 + cc

    def tok(yy, ll):
        return (yy % 4) * 2 + ll

    XL = (s, tok(y, 1 - l))
    YP, YM, Y2 = (s, tok(y + 1, l)), (s, tok(y + 3, l)), (s, tok(y + 2, l))
    ZP, ZM = (slot(z + 1, h, c), t), (slot(z + 3, h, c), t)
    XH, CO = (slot(z, 1 - h, c), t), (slot(z, h, 1 - c), t)
    NX, PV = ((s + 1) % 16, t), ((s + 15) % 16, t)

    def copy(src, dst, sem, dev):
        k = SEM[sem] if isinstance(sem, str) else sem
        return pltpu.make_async_remote_copy(
            src_ref=src, dst_ref=dst, send_sem=ss.at[k], recv_sem=rs.at[k], device_id=dev, device_id_type=MESH
        )

    sent = []

    def send(ref, sem, dev):
        cp = copy(ref, ref, sem, dev)
        cp.start()
        sent.append(cp)
        return cp

    barrier = pltpu.get_barrier_semaphore()
    here, before = (l + c) % 2, (l + 1 - c) % 2
    peers = [XL, YP, YM, Y2, ZP, ZM, XH, CO, NX, PV]
    peers += [(NX[0], tok(yy, here)) for yy in range(4)] + [(PV[0], tok(yy, before)) for yy in range(4)]
    for dev in peers:
        pl.semaphore_signal(barrier, inc=1, device_id=dev, device_id_type=MESH)

    def wrows(piece, first=0, size=PIECE):
        return w.at[pl.ds(pl.multiple_of(piece * PIECE + first, 32), size)]

    own = [
        pltpu.make_async_copy(
            wq.at[j], w.at[pl.ds(pl.multiple_of(s * PIECE, 64), PIECE), pl.ds(j * GROUP, GROUP)], local.at[j]
        )
        for j in range(3)
    ]
    for cp in own:
        cp.start()
    lv = level[0]
    factor = gain[...] * (1.0 + mod[lv, 0:1, :])
    offset = mod[lv, 1:2, :]

    def norm(i, _):
        rows = pl.ds(pl.multiple_of(i * 16, 16), 16)
        xf = lat[rows, :].astype(F32)
        mean = jnp.mean(xf, axis=-1, keepdims=True)
        centred = xf - mean
        var = jnp.mean(centred * centred, axis=-1, keepdims=True)
        x[t, rows, :] = (centred * lax.rsqrt(var + 1e-06) * factor + offset).astype(BF16)
        return 0

    lax.fori_loop(0, 4, norm, 0)
    for cp in own:
        cp.wait()
    pl.semaphore_wait(barrier, len(peers))

    yd = 2 * h + c
    gather = y == yd
    active = c == y % 2
    relay = active & (h != y // 2)

    def ocols(zz):
        return pl.ds(pl.multiple_of((zz % 4) * PIECE, 64), PIECE)

    def lanes(yy):
        return pl.ds(pl.multiple_of((yy % 4) * GROUP, 128), GROUP)

    def o_first():
        return copy(wo, wot.at[ocols(z), lanes(y)], SEM["o_a0"] + (y - yd + 4) % 4, (s, tok(yd, l)))

    def o_copy(name, dev, zz):
        ref = wot.at[ocols(zz)]
        return copy(ref, ref, name, dev)

    @pl.when(jnp.logical_not(gather))
    def _():
        o_first().start()

    @pl.when(gather)
    def _():
        cp = pltpu.make_async_copy(wo, wot.at[ocols(z), lanes(y)], local.at[3])
        cp.start()
        cp.wait()

    mine = wrows(s)
    w_xh = send(mine, "w_xh", XH)
    w_zp0 = send(mine, "w_zp0", ZP)
    w_zm0 = send(mine, "w_zm0", ZM)
    w_co = [send(mine, "w_co0", CO)]

    def shard(tt, half):
        return x.at[tt, pl.ds(half * HALF, HALF)]

    t_x, t_yp, t_ym = [], [], []
    for half in range(2):
        if half == 1:
            lax.fori_loop(4, 8, norm, 0)
        t_yp.append(send(shard(t, half), "t_yp%d" % half, YP))
        t_ym.append(send(shard(t, half), "t_ym%d" % half, YM))
        t_x.append(send(shard(t, half), "t_x%d" % half, XL))

    @pl.when(c == 0)
    def _():
        copy(lat, lat_prev, LAT, NX).start()

    def lat_copy(d):
        return copy(latc.at[(y + d) % 4], latr.at[y], LAT_Y + d, (s, tok(y + d, l)))

    def spread_latents():
        for yy in range(4):
            for zz in range(4):
                first = zz * COLS + yy * PIECE
                latc[yy, :, zz * PIECE:(zz + 1) * PIECE] = lat[:, first:first + PIECE]
        latr[y] = latc[y]

    pl.when(c == 1)(spread_latents)

    tm, tp, tx = tok(y + 3, l), tok(y + 1, l), tok(y, 1 - l)
    t2 = tok(y + 2, l)
    um, up, u2 = tok(y + 3, 1 - l), tok(y + 1, 1 - l), tok(y + 2, 1 - l)

    @pl.when(gather)
    def _():
        for d in range(1, 4):
            src = wot.at[ocols(z), lanes(0)]
            copy(src, src, SEM["o_a0"] + d, YP).wait_recv()
        o_copy("o_xh", XH, z).start()

    t_yp[0].wait_recv()
    t_fp = send(shard(tm, 0), "t_fp", YP)
    w_zp0.wait_recv()
    pm = slot(z + 3, h, c)
    w_fp0 = send(wrows(pm, 0, PIECE // 2), "w_fp0", ZP)
    w_co.append(send(wrows(pm), "w_co2", CO))
    w_zm0.wait_recv()
    pp = slot(z + 1, h, c)
    w_fm0 = send(wrows(pp, PIECE // 2, PIECE // 2), "w_fm0", ZM)
    w_co.append(send(wrows(pp), "w_co3", CO))
    w_xh.wait_recv()
    px = slot(z, 1 - h, c)
    w_zp1 = send(wrows(px), "w_zp1", ZP)
    w_zm1 = send(wrows(px), "w_zm1", ZM)
    w_co.append(send(wrows(px), "w_co1", CO))
    u_yp, u_ym = [], []

    def second(half):
        t_x[half].wait_recv()
        u_yp.append(send(shard(tx, half), "u_yp%d" % half, YP))
        u_ym.append(send(shard(tx, half), "u_ym%d" % half, YM))

    second(0)
    t_ym[1].wait_recv()
    t_fm = send(shard(tp, 1), "t_fm", YM)
    second(1)

    w_zp1.wait_recv()
    pm1 = slot(z + 3, 1 - h, c)
    w_fp1 = send(wrows(pm1, 0, PIECE // 2), "w_fp1", ZP)
    w_co.append(send(wrows(pm1), "w_co4", CO))
    w_zm1.wait_recv()
    pp1 = slot(z + 1, 1 - h, c)
    w_fm1 = send(wrows(pp1, PIECE // 2, PIECE // 2), "w_fm1", ZM)
    w_co.append(send(wrows(pp1), "w_co5", CO))

    def spread():
        for name, dev in (("o_zp", ZP), ("o_zm", ZM), ("o_co0", CO)):
            o_copy(name, dev, z).start()

    @pl.when(relay)
    def _():
        o_copy("o_xh", XH, z).wait_recv()

    @pl.when(active)
    def _():
        spread()

    w_fp0.wait_recv()
    w_fm0.wait_recv()
    w_co.append(send(wrows(slot(z + 2, h, c)), "w_co6", CO))
    t_fm.wait_recv()
    u_x = send(shard(t2, 1), "u_x", XL)

    w_fp1.wait_recv()
    w_fm1.wait_recv()
    w_co.append(send(wrows(slot(z + 2, 1 - h, c)), "w_co7", CO))
    for cp in w_co:
        cp.wait_recv()

    def quarter(tt, part):
        return x.at[tt, pl.ds(part * 32, 32)]

    def u_forward():
        a, b = quarter(um, 0), quarter(up, 1)
        return copy(a, a, "u_fp", YP), copy(b, b, "u_fm", YM)

    def kv_copy(tt, half, k):
        rows = pl.ds(pl.multiple_of(half * HALF, HALF), HALF)
        return copy(ctx.at[tt, rows], ctx.at[8 + tt, rows], KV0 + k, NX)

    def project(b, _):
        @pl.when(b == 1)
        def _():
            @pl.when(active)
            def _():
                o_copy("o_zm", ZM, z + 1).wait_recv()
                o_copy("o_z2", ZM, z + 1).start()

            t_yp[1].wait_recv()
            t_ym[0].wait_recv()

        @pl.when(b == 2)
        def _():
            t_fp.wait_recv()

        def pick(values):
            return jnp.where(b == 0, values[0], jnp.where(b == 1, values[1], values[2]))

        parts = [
            (pick((t, tm, um)), 0),
            (pick((t, tm, up)), pick((1, 1, 0))),
            (pick((tx, tp, t2)), 0),
            (pick((tx, tp, t2)), 1),
        ]
        compute(parts, 4 * b)
        return 0

    def compute(parts, first):
        parts = [(tt, half, pl.ds(pl.multiple_of(half * HALF, HALF), HALF)) for tt, half in parts]
        rows = jnp.concatenate([x[tt, rr, :] for tt, half, rr in parts], axis=0)
        for n in range(3):
            cols = slice(n * NTILE, (n + 1) * NTILE)
            part = jnp.dot(rows, w[:, GROUP + n * NTILE:GROUP + (n + 1) * NTILE], preferred_element_type=F32).astype(BF16)
            for i, (tt, half, rr) in enumerate(parts):
                ctx[tt, rr, cols] = part[i * HALF:(i + 1) * HALF]
        for i, (tt, half, rr) in enumerate(parts):
            kv_copy(tt, half, first + i).start()
        part = jnp.dot(rows, w[:, :GROUP], preferred_element_type=F32).astype(BF16)
        for i, (tt, half, rr) in enumerate(parts):
            q[tt, rr, :] = part[i * HALF:(i + 1) * HALF]

    u_yp[0].wait_recv()
    u_ym[0].wait_recv()
    for cp in u_forward():
        cp.start()

    @pl.when(c == 1)
    def _():
        for d in (1, 3, 2):
            lat_copy(d).start()

    lax.fori_loop(0, 3, project, 0)
    u_yp[1].wait_recv()
    u_ym[1].wait_recv()
    u_x.wait_recv()
    compute([(um, 1), (up, 1), (u2, 1)], 12)
    for cp in u_forward():
        cp.wait_recv()
    compute([(u2, 0)], 15)

    for k in range(16):
        kv_copy(t, 0, k).wait_recv()

    @pl.when(active)
    def _():
        for name, dz, onward in (("o_zp", 3, "o_co1"), ("o_zm", 1, "o_co2"), ("o_z2", 2, "o_co3")):
            if name != "o_zm":
                o_copy(name, ZP, z + dz).wait_recv()
            o_copy(onward, CO, z + dz).start()

    scale = 1.0 / math.sqrt(HD)

    def tile_at(yt, second_half):
        return 2 * (yt % 4) + jnp.where(second_half, here, 1 - here)

    def a_copy(j, late, base):
        if base == A_YP:
            ref, dev = att.at[tile_at(y + 1 + j, late), :, lanes(y)], YP
        elif base == A_YM:
            ref, dev = att.at[tile_at(y + 1 + j, late), :, lanes(y)], YM
        elif base == A_FP:
            ref, dev = att.at[tile_at(y + j, late), pl.ds(0, HALF), lanes(y + 3)], YP
        else:
            ref, dev = att.at[tile_at(y + 2 + j, late), pl.ds(HALF, HALF), lanes(y + 1)], YM
        return copy(ref, ref, base + j + jnp.where(late, 4, 0), dev)

    def at(k, values):
        return jnp.where(k == 0, values[0], jnp.where(k == 1, values[1], jnp.where(k == 2, values[2], values[3])))

    def attend(i):
        listed = [ids[j, i] for j in range(4)]
        valid = []
        for j in range(4):
            ok = j < counts[i]
            for e in range(j):
                ok = ok & (listed[e] != listed[j])
            valid.append(ok)
        outs = []
        ones = jnp.ones((4 * BLK, HD), BF16)
        for head in range(3):
            hc = slice(head * HD, (head + 1) * HD)
            vc = slice(GROUP + head * HD, GROUP + (head + 1) * HD)
            keys = jnp.concatenate([ctx[listed[j], :, hc] for j in range(4)], axis=0)
            scores = lax.dot_general(q[i, :, hc], keys, (((1,), (1,)), ((), ())), preferred_element_type=F32)
            scores = [jnp.where(valid[j], scores[:, j * BLK:(j + 1) * BLK], -1e30) for j in range(4)]
            top = jnp.maximum(jnp.maximum(scores[0], scores[1]), jnp.maximum(scores[2], scores[3]))
            top = jnp.max(top, axis=1, keepdims=True)
            probs = jnp.concatenate([jnp.exp((sc - top) * scale).astype(BF16) for sc in scores], axis=1)
            values = jnp.concatenate([ctx[listed[j], :, vc] for j in range(4)], axis=0)
            sums = jnp.dot(probs, jnp.concatenate([values, ones], axis=1), preferred_element_type=F32)
            outs.append((sums[:, :HD] / sums[:, HD:]).astype(BF16))
        att[i, :, lanes(y)] = jnp.concatenate(outs, axis=1)

    def onward_p(j, late):
        a_copy(j, late, A_YP).wait_recv()
        a_copy(j, late, A_FP).start()

    def onward_m(j, late):
        a_copy(j, late, A_YM).wait_recv()
        a_copy(j, late, A_FM).start()

    def attention(k, _):
        late = k >= 4
        attend(tile_at(y + 1 + at(k % 4, ORDER), late))

        @pl.when(k == 0)
        def _():
            a_copy(2, False, A_YP).start()
            a_copy(2, False, A_YM).start()

        @pl.when(k == 1)
        def _():
            a_copy(1, False, A_YP).start()

        @pl.when(k == 2)
        def _():
            a_copy(3, False, A_YM).start()

        @pl.when(k == 5)
        def _():
            onward_p(2, False)
            onward_m(2, False)
            a_copy(3, False, A_YP).start()
            a_copy(0, False, A_YM).start()
            a_copy(0, False, A_YP).start()
            a_copy(1, False, A_YM).start()

        return 0

    lax.fori_loop(0, 8, attention, 0)

    CORE = ("o_co0", "o_co1", "o_co2", "o_co3")

    @pl.when(jnp.logical_not(active))
    def _():
        for name in CORE:
            o_copy(name, CO, z).wait_recv()

    def turn(r, _):
        rows = pl.ds(pl.multiple_of(r * 128, 128), 128)
        wout[:, rows] = wot[rows, :].T
        return 0

    lax.fori_loop(0, 10, turn, 0)

    def product(p, late):
        j = (p + 2) % 4
        a_copy(j, late, A_FP).wait_recv()
        a_copy(j, late, A_FM).wait_recv()
        return jnp.dot(att[tile_at(y + 1 + p, late)], wout[...], preferred_element_type=F32)

    def p_copy(p):
        return copy(psend.at[p], precv.at[p], P_X + p, XL)

    def foreign(p):
        mine = product(p, False)

        @pl.when(c == 0)
        def _():
            psend[p] = mine.astype(BF16)

        @pl.when(c == 1)
        def _():
            psend[p] = (mine + latr[(y + 1 + p) % 4].astype(F32)).astype(BF16)

        p_copy(p).start()

    def late_sends(*tiles):
        for j in tiles:
            a_copy(j, True, A_YP).start()
            a_copy(j, True, A_YM).start()

    @pl.when(c == 1)
    def _():
        for d in (1, 2, 3):
            lat_copy(d).wait_recv()

    onward_p(1, False)
    onward_m(3, False)
    foreign(0)
    onward_p(3, False)
    onward_m(0, False)
    late_sends(2, 1)
    foreign(1)
    onward_p(0, False)
    onward_m(1, False)
    late_sends(3, 0)
    foreign(2)
    foreign(3)
    for j in ORDER:
        onward_p(j, True)
        onward_m(j, True)

    def s_copy(p):
        return copy(ssend.at[p], branch.at[y], S_Y + p, (NX[0], tok(y + 1 + p, here)))

    def finish(p, _):
        mine = product(p, True)
        p_copy(p).wait_recv()
        ssend[p] = (mine + precv[p].astype(F32)).astype(BF16)
        s_copy(p).start()
        return 0

    lax.fori_loop(0, 4, finish, 0)

    for cp in sent:
        cp.wait_send()
    for cp in u_forward():
        cp.wait_send()

    def drain(k, _):
        kv_copy(t, 0, 2 * k).wait_send()
        kv_copy(t, 0, 2 * k + 1).wait_send()
        for base in (A_YP, A_YM, A_FP, A_FM):
            a_copy(k % 4, k >= 4, base).wait_send()
        return 0

    lax.fori_loop(0, 8, drain, 0)
    for p in range(4):
        p_copy(p).wait_send()
        s_copy(p).wait_send()

    @pl.when(c == 0)
    def _():
        copy(lat, lat_prev, LAT, NX).wait_send()

    @pl.when(c == 1)
    def _():
        for d in (1, 2, 3):
            lat_copy(d).wait_send()


    @pl.when(jnp.logical_not(gather))
    def _():
        o_first().wait_send()

    @pl.when(gather)
    def _():
        o_copy("o_xh", XH, z).wait_send()

    @pl.when(active)
    def _():
        for name in ("o_zp", "o_zm", "o_z2") + CORE:
            o_copy(name, CO, z).wait_send()


    @pl.when(c == 1)
    def _():
        copy(lat, lat_prev, LAT, NX).wait_recv()

    for p in range(4):
        s_copy(p).wait_recv()


def residual(branch, lat, out):
    add = lax.axis_index("slot") % 2 == 1
    for zz in range(4):
        cols = slice(zz * COLS, (zz + 1) * COLS)
        pieces = [branch[yy, :, zz * PIECE:(zz + 1) * PIECE] for yy in range(4)]
        base = jnp.where(add, lat[:, cols].astype(F32), 0.0)
        out[:, cols] = (base + jnp.concatenate(pieces, axis=1).astype(F32)).astype(BF16)


def body(latents, gain, mod_table, slot_noise_level, key_block_index, counts, w_qkv, w_out):
    vmem = pl.BlockSpec(memory_space=pltpu.VMEM)
    smem = pl.BlockSpec(memory_space=pltpu.SMEM)
    hbm = pl.BlockSpec(memory_space=pl.ANY)
    blocks = pltpu.VMEM((4, ROWS, COLS), BF16)
    branch, lat_prev = pl.pallas_call(
        kernel,
        out_shape=[jax.ShapeDtypeStruct((4, ROWS, COLS), BF16), jax.ShapeDtypeStruct((ROWS, D), BF16)],
        in_specs=[vmem, vmem, vmem, smem, smem, smem, hbm, hbm],
        out_specs=[hbm, hbm],
        scratch_shapes=[
            pltpu.VMEM((8, ROWS, D), BF16),
            pltpu.VMEM((D, QKV), BF16),
            pltpu.VMEM((COLS, 4 * GROUP), BF16),
            pltpu.VMEM((4 * GROUP, COLS), BF16),
            pltpu.VMEM((8, ROWS, GROUP), BF16),
            pltpu.VMEM((16, ROWS, 2 * GROUP), BF16),
            pltpu.VMEM((8, ROWS, 4 * GROUP), BF16),
            blocks,
            blocks,
            blocks,
            blocks,
            blocks,
            pltpu.SemaphoreType.DMA((4,)),
            pltpu.SemaphoreType.DMA((N_SEM,)),
            pltpu.SemaphoreType.DMA((N_SEM,)),
        ],
        compiler_params=pltpu.CompilerParams(
            collective_id=0, has_side_effects=True, vmem_limit_bytes=60 * 2**20
        ),
        name="window",
    )(latents[0], gain[None], mod_table, slot_noise_level, key_block_index[0].T, counts[0], w_qkv, w_out.T)
    out = pl.pallas_call(
        residual,
        grid=(2,),
        out_shape=jax.ShapeDtypeStruct((ROWS, D), BF16),
        in_specs=[pl.BlockSpec((4, ROWS // 2, COLS), lambda i: (0, i, 0)), pl.BlockSpec((ROWS // 2, D), lambda i: (i, 0))],
        out_specs=pl.BlockSpec((ROWS // 2, D), lambda i: (i, 0)),
        name="residual",
    )(branch, lat_prev)
    return out[None]


def solution(mesh):
    in_specs = (
        P("slot", "tok", None),
        P(),
        P(),
        P("slot"),
        P("slot", None, None),
        P("slot", None),
        P(None, "slot", "tok"),
        P("tok", "slot"),
    )
    out_specs = P("slot", "tok", None)
    return jax.shard_map(body, mesh=mesh, in_specs=in_specs, out_specs=out_specs, check_vma=False)
```

```python
import functools
import math

import jax
import jax.numpy as jnp
from jax import lax
from jax.experimental import pallas as pl
from jax.experimental.pallas import tpu as pltpu
from jax.sharding import PartitionSpec as P

MESH = pl.DeviceIdType.MESH
BF16 = jnp.bfloat16
F32 = jnp.float32

HD = 128
BLK = 128
ROWS = 128
D = 5120
QKV = 1152
PIECE = 320
HALF = 64
NTILE = 256
COLS = 1280
GROUP = 384

NAMES = (
    "w_xh", "w_zp0", "w_zm0", "w_co0", "w_zp1", "w_zm1", "w_co1", "w_fp0", "w_fm0", "w_co2", "w_co3",
    "w_fp1", "w_fm1", "w_co4", "w_co5", "w_co6", "w_co7", "t_x0", "t_x1", "t_yp0", "t_yp1", "t_ym0", "t_ym1",
    "t_fp", "t_fm", "u_yp0", "u_yp1", "u_ym0", "u_ym1", "u_fp", "u_fm", "u_x", "o_a0", "o_a1", "o_a2",
    "o_a3", "o_xh", "o_zp", "o_zm", "o_z2", "o_co0", "o_co1", "o_co2", "o_co3",
)
SEM = {name: i for i, name in enumerate(NAMES)}
KV0 = len(NAMES)
A_YP = KV0 + 16
A_YM = A_YP + 8
A_FP = A_YM + 8
A_FM = A_FP + 8
P_X = A_FM + 8
S_Y = P_X + 4
LAT = S_Y + 4
LAT_Y = LAT + 1
N_SEM = LAT_Y + 4
ORDER = (2, 1, 3, 0)


def kernel(lat_in, gain, mod_in, level, ids, counts, wq, wo, branch, lat_prev,
           x, w, wot, wout, q, ctx, att, psend, precv, ssend, latc, latr, lat, mod, local, go, ss, rs):
    s, t = lax.axis_index("slot"), lax.axis_index("tok")
    z, h, c = s // 4, (s // 2) % 2, s % 2
    y, l = t // 2, t % 2

    def slot(zz, hh, cc):
        return (zz % 4) * 4 + hh * 2 + cc

    def tok(yy, ll):
        return (yy % 4) * 2 + ll

    XL = (s, tok(y, 1 - l))
    YP, YM, Y2 = (s, tok(y + 1, l)), (s, tok(y + 3, l)), (s, tok(y + 2, l))
    ZP, ZM = (slot(z + 1, h, c), t), (slot(z + 3, h, c), t)
    XH, CO = (slot(z, 1 - h, c), t), (slot(z, h, 1 - c), t)
    NX, PV = ((s + 1) % 16, t), ((s + 15) % 16, t)

    def copy(src, dst, sem, dev):
        k = SEM[sem] if isinstance(sem, str) else sem
        return pltpu.make_async_remote_copy(
            src_ref=src, dst_ref=dst, send_sem=ss.at[k], recv_sem=rs.at[k], device_id=dev, device_id_type=MESH
        )

    sent = []

    def send(ref, sem, dev):
        cp = copy(ref, ref, sem, dev)
        cp.start()
        sent.append(cp)
        return cp

    inputs = [pltpu.make_async_copy(lat_in, lat, local.at[4]), pltpu.make_async_copy(mod_in, mod, local.at[5])]
    for cp in inputs:
        cp.start()
    barrier = pltpu.get_barrier_semaphore()
    here, before = (l + c) % 2, (l + 1 - c) % 2
    peers = [XL, YP, YM, Y2, ZP, ZM, XH, CO, NX, PV]
    peers += [(NX[0], tok(yy, here)) for yy in range(4)] + [(PV[0], tok(yy, before)) for yy in range(4)]
    for dev in peers:
        pl.semaphore_signal(barrier, inc=1, device_id=dev, device_id_type=MESH)

    def wrows(piece, first=0, size=PIECE):
        return w.at[pl.ds(pl.multiple_of(piece * PIECE + first, 32), size)]

    own = [
        pltpu.make_async_copy(
            wq.at[j], w.at[pl.ds(pl.multiple_of(s * PIECE, 64), PIECE), pl.ds(j * GROUP, GROUP)], local.at[j]
        )
        for j in range(3)
    ]
    for cp in own:
        cp.start()
    for cp in inputs:
        cp.wait()
    lv = level[0]
    factor = gain[...] * (1.0 + mod[lv, 0:1, :])
    offset = mod[lv, 1:2, :]

    def norm(i, _):
        rows = pl.ds(pl.multiple_of(i * 16, 16), 16)
        xf = lat[rows, :].astype(F32)
        mean = jnp.mean(xf, axis=-1, keepdims=True)
        centred = xf - mean
        var = jnp.mean(centred * centred, axis=-1, keepdims=True)
        x[t, rows, :] = (centred * lax.rsqrt(var + 1e-06) * factor + offset).astype(BF16)
        return 0

    lax.fori_loop(0, 4, norm, 0)
    for cp in own:
        cp.wait()
    pl.semaphore_wait(barrier, len(peers))

    yd = 2 * h + c
    gather = y == yd
    active = c == y % 2
    relay = active & (h != y // 2)

    def ocols(zz):
        return pl.ds(pl.multiple_of((zz % 4) * PIECE, 64), PIECE)

    def lanes(yy):
        return pl.ds(pl.multiple_of((yy % 4) * GROUP, 128), GROUP)

    def o_first():
        return copy(wo, wot.at[ocols(z), lanes(y)], SEM["o_a0"] + (y - yd + 4) % 4, (s, tok(yd, l)))

    def o_copy(name, dev, zz):
        ref = wot.at[ocols(zz)]
        return copy(ref, ref, name, dev)

    @pl.when(jnp.logical_not(gather))
    def _():
        o_first().start()

    @pl.when(gather)
    def _():
        cp = pltpu.make_async_copy(wo, wot.at[ocols(z), lanes(y)], local.at[3])
        cp.start()
        cp.wait()

    mine = wrows(s)
    w_xh = send(mine, "w_xh", XH)
    w_zp0 = send(mine, "w_zp0", ZP)
    w_zm0 = send(mine, "w_zm0", ZM)
    w_co = [send(mine, "w_co0", CO)]

    def shard(tt, half):
        return x.at[tt, pl.ds(half * HALF, HALF)]

    t_x, t_yp, t_ym = [], [], []
    for half in range(2):
        if half == 1:
            lax.fori_loop(4, 8, norm, 0)
        if half == 0:
            t_x.append(send(shard(t, half), "t_x%d" % half, XL))

            @pl.when(c == 0)
            def _():
                pl.semaphore_wait(go, 1)

        t_yp.append(send(shard(t, half), "t_yp%d" % half, YP))
        t_ym.append(send(shard(t, half), "t_ym%d" % half, YM))

    @pl.when(c == 1)
    def _():
        t_yp[0].wait_send()
        pl.semaphore_signal(go, inc=1, device_id=CO, device_id_type=MESH)

    @pl.when(c == 0)
    def _():
        copy(lat, lat_prev, LAT, NX).start()

    def lat_copy(d):
        return copy(latc.at[(y + d) % 4], latr.at[y], LAT_Y + d, (s, tok(y + d, l)))

    def spread_latents():
        for yy in range(4):
            for zz in range(4):
                first = zz * COLS + yy * PIECE
                latc[yy, :, zz * PIECE:(zz + 1) * PIECE] = lat[:, first:first + PIECE]
        latr[y] = latc[y]

    pl.when(c == 1)(spread_latents)

    tm, tp, tx = tok(y + 3, l), tok(y + 1, l), tok(y, 1 - l)
    t2 = tok(y + 2, l)
    um, up, u2 = tok(y + 3, 1 - l), tok(y + 1, 1 - l), tok(y + 2, 1 - l)

    @pl.when(gather)
    def _():
        for d in range(1, 4):
            src = wot.at[ocols(z), lanes(0)]
            copy(src, src, SEM["o_a0"] + d, YP).wait_recv()
        o_copy("o_xh", XH, z).start()

    t_x.append(send(shard(t, 1), "t_x1", XL))
    t_yp[0].wait_recv()
    t_fp = send(shard(tm, 0), "t_fp", YP)
    w_zp0.wait_recv()
    pm = slot(z + 3, h, c)
    w_fp0 = send(wrows(pm, 0, PIECE // 2), "w_fp0", ZP)
    w_co.append(send(wrows(pm), "w_co2", CO))
    w_zm0.wait_recv()
    pp = slot(z + 1, h, c)
    w_fm0 = send(wrows(pp, PIECE // 2, PIECE // 2), "w_fm0", ZM)
    w_co.append(send(wrows(pp), "w_co3", CO))
    w_xh.wait_recv()
    px = slot(z, 1 - h, c)
    w_zp1 = send(wrows(px), "w_zp1", ZP)
    w_zm1 = send(wrows(px), "w_zm1", ZM)
    w_co.append(send(wrows(px), "w_co1", CO))
    u_yp, u_ym = [], []

    def second(half):
        t_x[half].wait_recv()
        u_yp.append(send(shard(tx, half), "u_yp%d" % half, YP))
        u_ym.append(send(shard(tx, half), "u_ym%d" % half, YM))

    second(0)
    t_ym[1].wait_recv()
    t_fm = send(shard(tp, 1), "t_fm", YM)
    second(1)

    w_zp1.wait_recv()
    pm1 = slot(z + 3, 1 - h, c)
    w_fp1 = send(wrows(pm1, 0, PIECE // 2), "w_fp1", ZP)
    w_co.append(send(wrows(pm1), "w_co4", CO))
    w_zm1.wait_recv()
    pp1 = slot(z + 1, 1 - h, c)
    w_fm1 = send(wrows(pp1, PIECE // 2, PIECE // 2), "w_fm1", ZM)
    w_co.append(send(wrows(pp1), "w_co5", CO))

    def spread():
        for name, dev in (("o_zp", ZP), ("o_zm", ZM), ("o_co0", CO)):
            o_copy(name, dev, z).start()

    @pl.when(relay)
    def _():
        o_copy("o_xh", XH, z).wait_recv()

    @pl.when(active)
    def _():
        spread()

    w_fp0.wait_recv()
    w_fm0.wait_recv()
    w_co.append(send(wrows(slot(z + 2, h, c)), "w_co6", CO))
    t_fm.wait_recv()
    u_x = send(shard(t2, 1), "u_x", XL)

    w_fp1.wait_recv()
    w_fm1.wait_recv()
    w_co.append(send(wrows(slot(z + 2, 1 - h, c)), "w_co7", CO))
    for cp in w_co:
        cp.wait_recv()

    def quarter(tt, part):
        return x.at[tt, pl.ds(part * 32, 32)]

    def u_forward():
        a, b = quarter(um, 0), quarter(up, 1)
        return copy(a, a, "u_fp", YP), copy(b, b, "u_fm", YM)

    def kv_copy(tt, half, k):
        rows = pl.ds(pl.multiple_of(half * HALF, HALF), HALF)
        return copy(ctx.at[tt, rows], ctx.at[8 + tt, rows], KV0 + k, NX)

    def project(b, _):
        @pl.when(b == 1)
        def _():
            @pl.when(active)
            def _():
                o_copy("o_zm", ZM, z + 1).wait_recv()
                o_copy("o_z2", ZM, z + 1).start()

            t_yp[1].wait_recv()
            t_ym[0].wait_recv()

        @pl.when(b == 2)
        def _():
            t_fp.wait_recv()

        def pick(values):
            return jnp.where(b == 0, values[0], jnp.where(b == 1, values[1], values[2]))

        parts = [
            (pick((t, tm, um)), 0),
            (pick((t, tm, up)), pick((1, 1, 0))),
            (pick((tx, tp, t2)), 0),
            (pick((tx, tp, t2)), 1),
        ]
        compute(parts, 4 * b)
        return 0

    def compute(parts, first):
        parts = [(tt, half, pl.ds(pl.multiple_of(half * HALF, HALF), HALF)) for tt, half in parts]
        rows = jnp.concatenate([x[tt, rr, :] for tt, half, rr in parts], axis=0)
        for n in range(3):
            cols = slice(n * NTILE, (n + 1) * NTILE)
            part = jnp.dot(rows, w[:, GROUP + n * NTILE:GROUP + (n + 1) * NTILE], preferred_element_type=F32).astype(BF16)
            for i, (tt, half, rr) in enumerate(parts):
                ctx[tt, rr, cols] = part[i * HALF:(i + 1) * HALF]
        for i, (tt, half, rr) in enumerate(parts):
            kv_copy(tt, half, first + i).start()
        part = jnp.dot(rows, w[:, :GROUP], preferred_element_type=F32).astype(BF16)
        for i, (tt, half, rr) in enumerate(parts):
            q[tt, rr, :] = part[i * HALF:(i + 1) * HALF]

    u_yp[0].wait_recv()
    u_ym[0].wait_recv()
    for cp in u_forward():
        cp.start()

    @pl.when(c == 1)
    def _():
        for d in (1, 3, 2):
            lat_copy(d).start()

    lax.fori_loop(0, 3, project, 0)
    u_yp[1].wait_recv()
    u_ym[1].wait_recv()
    u_x.wait_recv()
    compute([(um, 1), (up, 1), (u2, 1)], 12)
    for cp in u_forward():
        cp.wait_recv()
    compute([(u2, 0)], 15)

    for k in range(16):
        kv_copy(t, 0, k).wait_recv()

    @pl.when(active)
    def _():
        for name, dz, onward in (("o_zp", 3, "o_co1"), ("o_zm", 1, "o_co2"), ("o_z2", 2, "o_co3")):
            if name != "o_zm":
                o_copy(name, ZP, z + dz).wait_recv()
            o_copy(onward, CO, z + dz).start()

    scale = 1.0 / math.sqrt(HD)

    def tile_at(yt, second_half):
        return 2 * (yt % 4) + jnp.where(second_half, here, 1 - here)

    def a_copy(j, late, base):
        if base == A_YP:
            ref, dev = att.at[tile_at(y + 1 + j, late), :, lanes(y)], YP
        elif base == A_YM:
            ref, dev = att.at[tile_at(y + 1 + j, late), :, lanes(y)], YM
        elif base == A_FP:
            ref, dev = att.at[tile_at(y + j, late), pl.ds(0, HALF), lanes(y + 3)], YP
        else:
            ref, dev = att.at[tile_at(y + 2 + j, late), pl.ds(HALF, HALF), lanes(y + 1)], YM
        return copy(ref, ref, base + j + jnp.where(late, 4, 0), dev)

    def at(k, values):
        return jnp.where(k == 0, values[0], jnp.where(k == 1, values[1], jnp.where(k == 2, values[2], values[3])))

    def attend(i):
        listed = [ids[j, i] for j in range(4)]
        valid = []
        for j in range(4):
            ok = j < counts[i]
            for e in range(j):
                ok = ok & (listed[e] != listed[j])
            valid.append(ok)
        outs = []
        ones = jnp.ones((4 * BLK, HD), BF16)
        for head in range(3):
            hc = slice(head * HD, (head + 1) * HD)
            vc = slice(GROUP + head * HD, GROUP + (head + 1) * HD)
            keys = jnp.concatenate([ctx[listed[j], :, hc] for j in range(4)], axis=0)
            scores = lax.dot_general(q[i, :, hc], keys, (((1,), (1,)), ((), ())), preferred_element_type=F32)
            scores = [jnp.where(valid[j], scores[:, j * BLK:(j + 1) * BLK], -1e30) for j in range(4)]
            top = jnp.maximum(jnp.maximum(scores[0], scores[1]), jnp.maximum(scores[2], scores[3]))
            top = jnp.max(top, axis=1, keepdims=True)
            probs = jnp.concatenate([jnp.exp((sc - top) * scale).astype(BF16) for sc in scores], axis=1)
            values = jnp.concatenate([ctx[listed[j], :, vc] for j in range(4)], axis=0)
            sums = jnp.dot(probs, jnp.concatenate([values, ones], axis=1), preferred_element_type=F32)
            outs.append((sums[:, :HD] / sums[:, HD:]).astype(BF16))
        att[i, :, lanes(y)] = jnp.concatenate(outs, axis=1)

    def onward_p(j, late):
        a_copy(j, late, A_YP).wait_recv()
        a_copy(j, late, A_FP).start()

    def onward_m(j, late):
        a_copy(j, late, A_YM).wait_recv()
        a_copy(j, late, A_FM).start()

    def attention(k, _):
        late = k >= 4
        attend(tile_at(y + 1 + at(k % 4, ORDER), late))

        @pl.when(k == 0)
        def _():
            a_copy(2, False, A_YP).start()
            a_copy(2, False, A_YM).start()

        @pl.when(k == 1)
        def _():
            a_copy(1, False, A_YP).start()

        @pl.when(k == 2)
        def _():
            a_copy(3, False, A_YM).start()

        @pl.when(k == 5)
        def _():
            onward_p(2, False)
            onward_m(2, False)
            a_copy(3, False, A_YP).start()
            a_copy(0, False, A_YM).start()
            a_copy(0, False, A_YP).start()
            a_copy(1, False, A_YM).start()

        return 0

    lax.fori_loop(0, 8, attention, 0)

    CORE = ("o_co0", "o_co1", "o_co2", "o_co3")

    @pl.when(jnp.logical_not(active))
    def _():
        for name in CORE:
            o_copy(name, CO, z).wait_recv()

    def turn(r, _):
        rows = pl.ds(pl.multiple_of(r * 128, 128), 128)
        wout[:, rows] = wot[rows, :].T
        return 0

    lax.fori_loop(0, 10, turn, 0)

    def product(p, late):
        j = (p + 2) % 4
        a_copy(j, late, A_FP).wait_recv()
        a_copy(j, late, A_FM).wait_recv()
        return jnp.dot(att[tile_at(y + 1 + p, late)], wout[...], preferred_element_type=F32)

    def p_copy(p):
        return copy(psend.at[p], precv.at[p], P_X + p, XL)

    def foreign(p):
        mine = product(p, False)

        @pl.when(c == 0)
        def _():
            psend[p] = mine.astype(BF16)

        @pl.when(c == 1)
        def _():
            psend[p] = (mine + latr[(y + 1 + p) % 4].astype(F32)).astype(BF16)

        p_copy(p).start()

    def late_sends(*tiles):
        for j in tiles:
            a_copy(j, True, A_YP).start()
            a_copy(j, True, A_YM).start()

    @pl.when(c == 1)
    def _():
        for d in (1, 2, 3):
            lat_copy(d).wait_recv()

    onward_p(1, False)
    onward_m(3, False)
    foreign(0)
    onward_p(3, False)
    onward_m(0, False)
    late_sends(2, 1)
    foreign(1)
    onward_p(0, False)
    onward_m(1, False)
    late_sends(3, 0)
    foreign(2)
    foreign(3)
    for j in ORDER:
        onward_p(j, True)
        onward_m(j, True)

    def s_copy(p):
        return copy(ssend.at[p], branch.at[y], S_Y + p, (NX[0], tok(y + 1 + p, here)))

    def finish(p, _):
        mine = product(p, True)
        p_copy(p).wait_recv()
        ssend[p] = (mine + precv[p].astype(F32)).astype(BF16)
        s_copy(p).start()
        return 0

    lax.fori_loop(0, 4, finish, 0)

    for cp in sent:
        if cp is not t_yp[0]:
            cp.wait_send()

    @pl.when(c == 0)
    def _():
        t_yp[0].wait_send()

    for cp in u_forward():
        cp.wait_send()

    def drain(k, _):
        kv_copy(t, 0, 2 * k).wait_send()
        kv_copy(t, 0, 2 * k + 1).wait_send()
        for base in (A_YP, A_YM, A_FP, A_FM):
            a_copy(k % 4, k >= 4, base).wait_send()
        return 0

    lax.fori_loop(0, 8, drain, 0)
    for p in range(4):
        p_copy(p).wait_send()
        s_copy(p).wait_send()

    @pl.when(c == 0)
    def _():
        copy(lat, lat_prev, LAT, NX).wait_send()

    @pl.when(c == 1)
    def _():
        for d in (1, 2, 3):
            lat_copy(d).wait_send()


    @pl.when(jnp.logical_not(gather))
    def _():
        o_first().wait_send()

    @pl.when(gather)
    def _():
        o_copy("o_xh", XH, z).wait_send()

    @pl.when(active)
    def _():
        for name in ("o_zp", "o_zm", "o_z2") + CORE:
            o_copy(name, CO, z).wait_send()


    @pl.when(c == 1)
    def _():
        copy(lat, lat_prev, LAT, NX).wait_recv()

    for p in range(4):
        s_copy(p).wait_recv()


def residual(branch, lat, out):
    add = lax.axis_index("slot") % 2 == 1
    for zz in range(4):
        cols = slice(zz * COLS, (zz + 1) * COLS)
        pieces = [branch[yy, :, zz * PIECE:(zz + 1) * PIECE] for yy in range(4)]
        base = jnp.where(add, lat[:, cols].astype(F32), 0.0)
        out[:, cols] = (base + jnp.concatenate(pieces, axis=1).astype(F32)).astype(BF16)


def body(latents, gain, mod_table, slot_noise_level, key_block_index, counts, w_qkv, w_out):
    vmem = pl.BlockSpec(memory_space=pltpu.VMEM)
    smem = pl.BlockSpec(memory_space=pltpu.SMEM)
    hbm = pl.BlockSpec(memory_space=pl.ANY)
    blocks = pltpu.VMEM((4, ROWS, COLS), BF16)
    branch, lat_prev = pl.pallas_call(
        kernel,
        out_shape=[jax.ShapeDtypeStruct((4, ROWS, COLS), BF16), jax.ShapeDtypeStruct((ROWS, D), BF16)],
        in_specs=[hbm, vmem, hbm, smem, smem, smem, hbm, hbm],
        out_specs=[hbm, hbm],
        scratch_shapes=[
            pltpu.VMEM((8, ROWS, D), BF16),
            pltpu.VMEM((D, QKV), BF16),
            pltpu.VMEM((COLS, 4 * GROUP), BF16),
            pltpu.VMEM((4 * GROUP, COLS), BF16),
            pltpu.VMEM((8, ROWS, GROUP), BF16),
            pltpu.VMEM((16, ROWS, 2 * GROUP), BF16),
            pltpu.VMEM((8, ROWS, 4 * GROUP), BF16),
            blocks,
            blocks,
            blocks,
            blocks,
            blocks,
            pltpu.VMEM((ROWS, D), BF16),
            pltpu.VMEM((16, 2, D), F32),
            pltpu.SemaphoreType.DMA((6,)),
            pltpu.SemaphoreType.REGULAR,
            pltpu.SemaphoreType.DMA((N_SEM,)),
            pltpu.SemaphoreType.DMA((N_SEM,)),
        ],
        compiler_params=pltpu.CompilerParams(
            collective_id=0, has_side_effects=True, vmem_limit_bytes=60 * 2**20
        ),
        name="window",
    )(latents[0], gain[None], mod_table, slot_noise_level, key_block_index[0].T, counts[0], w_qkv, w_out.T)
    out = pl.pallas_call(
        residual,
        grid=(2,),
        out_shape=jax.ShapeDtypeStruct((ROWS, D), BF16),
        in_specs=[pl.BlockSpec((4, ROWS // 2, COLS), lambda i: (0, i, 0)), pl.BlockSpec((ROWS // 2, D), lambda i: (i, 0))],
        out_specs=pl.BlockSpec((ROWS // 2, D), lambda i: (i, 0)),
        name="residual",
    )(branch, lat_prev)
    return out[None]


def solution(mesh):
    in_specs = (
        P("slot", "tok", None),
        P(),
        P(),
        P("slot"),
        P("slot", None, None),
        P("slot", None),
        P(None, "slot", "tok"),
        P("tok", "slot"),
    )
    out_specs = P("slot", "tok", None)
    return jax.shard_map(body, mesh=mesh, in_specs=in_specs, out_specs=out_specs, check_vma=False)
```

```python
import functools
import math

import jax
import jax.numpy as jnp
from jax import lax
from jax.experimental import pallas as pl
from jax.experimental.pallas import tpu as pltpu
from jax.sharding import PartitionSpec as P

MESH = pl.DeviceIdType.MESH
BF16 = jnp.bfloat16
F32 = jnp.float32

HD = 128
BLK = 128
ROWS = 128
D = 5120
QKV = 1152
PIECE = 320
HALF = 64
NTILE = 256
COLS = 1280
GROUP = 384

NAMES = (
    "w_xh", "w_zp0", "w_zm0", "w_co0", "w_zp1", "w_zm1", "w_co1", "w_fp0", "w_fm0", "w_co2", "w_co3",
    "w_fp1", "w_fm1", "w_co4", "w_co5", "w_co6", "w_co7", "t_x0", "t_x1", "t_yp0", "t_yp1", "t_ym0", "t_ym1",
    "t_fp", "t_fm", "u_yp0", "u_yp1", "u_ym0", "u_ym1", "u_fp", "u_fm", "u_x", "o_a0", "o_a1", "o_a2",
    "o_a3", "o_xh", "o_zp", "o_zm", "o_z2", "o_co0", "o_co1", "o_co2", "o_co3",
)
SEM = {name: i for i, name in enumerate(NAMES)}
KV0 = len(NAMES)
A_YP = KV0 + 16
A_YM = A_YP + 8
A_FP = A_YM + 8
A_FM = A_FP + 8
P_X = A_FM + 8
S_Y = P_X + 4
LAT = S_Y + 4
LAT_Y = LAT + 1
N_SEM = LAT_Y + 4
ORDER = (2, 1, 3, 0)


def kernel(lat_in, gain, mod_in, level, ids, counts, wq, wo, branch, lat_prev,
           x, w, wot, wout, q, ctx, att, psend, precv, ssend, latc, latr, lat, mod, local, go, ss, rs):
    s, t = lax.axis_index("slot"), lax.axis_index("tok")
    z, h, c = s // 4, (s // 2) % 2, s % 2
    y, l = t // 2, t % 2

    def slot(zz, hh, cc):
        return (zz % 4) * 4 + hh * 2 + cc

    def tok(yy, ll):
        return (yy % 4) * 2 + ll

    XL = (s, tok(y, 1 - l))
    YP, YM, Y2 = (s, tok(y + 1, l)), (s, tok(y + 3, l)), (s, tok(y + 2, l))
    ZP, ZM = (slot(z + 1, h, c), t), (slot(z + 3, h, c), t)
    XH, CO = (slot(z, 1 - h, c), t), (slot(z, h, 1 - c), t)
    NX, PV = ((s + 1) % 16, t), ((s + 15) % 16, t)

    def copy(src, dst, sem, dev):
        k = SEM[sem] if isinstance(sem, str) else sem
        return pltpu.make_async_remote_copy(
            src_ref=src, dst_ref=dst, send_sem=ss.at[k], recv_sem=rs.at[k], device_id=dev, device_id_type=MESH
        )

    sent = []

    def send(ref, sem, dev):
        cp = copy(ref, ref, sem, dev)
        cp.start()
        sent.append(cp)
        return cp

    inputs = [pltpu.make_async_copy(lat_in, lat, local.at[4]), pltpu.make_async_copy(mod_in, mod, local.at[5])]
    for cp in inputs:
        cp.start()
    barrier = pltpu.get_barrier_semaphore()
    here, before = (l + c) % 2, (l + 1 - c) % 2
    peers = [XL, YP, YM, Y2, ZP, ZM, XH, CO, NX, PV]
    peers += [(NX[0], tok(yy, here)) for yy in range(4)] + [(PV[0], tok(yy, before)) for yy in range(4)]
    for dev in peers:
        pl.semaphore_signal(barrier, inc=1, device_id=dev, device_id_type=MESH)

    def wrows(piece, first=0, size=PIECE):
        return w.at[pl.ds(pl.multiple_of(piece * PIECE + first, 32), size)]

    own = [
        pltpu.make_async_copy(
            wq.at[j], w.at[pl.ds(pl.multiple_of(s * PIECE, 64), PIECE), pl.ds(j * GROUP, GROUP)], local.at[j]
        )
        for j in range(3)
    ]
    for cp in own:
        cp.start()
    for cp in inputs:
        cp.wait()
    lv = level[0]
    factor = gain[...] * (1.0 + mod[lv, 0:1, :])
    offset = mod[lv, 1:2, :]

    def norm(i, _):
        rows = pl.ds(pl.multiple_of(i * 16, 16), 16)
        xf = lat[rows, :].astype(F32)
        mean = jnp.mean(xf, axis=-1, keepdims=True)
        centred = xf - mean
        var = jnp.mean(centred * centred, axis=-1, keepdims=True)
        x[t, rows, :] = (centred * lax.rsqrt(var + 1e-06) * factor + offset).astype(BF16)
        return 0

    lax.fori_loop(0, 4, norm, 0)
    for cp in own:
        cp.wait()
    pl.semaphore_wait(barrier, len(peers))

    yd = 2 * h + c
    gather = y == yd
    active = c == y % 2
    relay = active & (h != y // 2)

    def ocols(zz):
        return pl.ds(pl.multiple_of((zz % 4) * PIECE, 64), PIECE)

    def lanes(yy):
        return pl.ds(pl.multiple_of((yy % 4) * GROUP, 128), GROUP)

    def o_first():
        return copy(wo, wot.at[ocols(z), lanes(y)], SEM["o_a0"] + (y - yd + 4) % 4, (s, tok(yd, l)))

    def o_copy(name, dev, zz):
        ref = wot.at[ocols(zz)]
        return copy(ref, ref, name, dev)

    @pl.when(jnp.logical_not(gather))
    def _():
        o_first().start()

    @pl.when(gather)
    def _():
        cp = pltpu.make_async_copy(wo, wot.at[ocols(z), lanes(y)], local.at[3])
        cp.start()
        cp.wait()

    mine = wrows(s)
    w_xh = send(mine, "w_xh", XH)
    w_zp0 = send(mine, "w_zp0", ZP)
    w_zm0 = send(mine, "w_zm0", ZM)
    w_co = [send(mine, "w_co0", CO)]

    def shard(tt, half):
        return x.at[tt, pl.ds(half * HALF, HALF)]

    t_x, t_yp, t_ym = [], [], []
    for half in range(2):
        if half == 1:
            lax.fori_loop(4, 8, norm, 0)
        if half == 0:
            t_x.append(send(shard(t, half), "t_x%d" % half, XL))

            @pl.when(c == 0)
            def _():
                pl.semaphore_wait(go, 1)

        t_yp.append(send(shard(t, half), "t_yp%d" % half, YP))
        t_ym.append(send(shard(t, half), "t_ym%d" % half, YM))

    @pl.when(c == 1)
    def _():
        t_yp[0].wait_send()
        pl.semaphore_signal(go, inc=1, device_id=CO, device_id_type=MESH)

    @pl.when(c == 0)
    def _():
        copy(lat, lat_prev, LAT, NX).start()

    def lat_copy(d):
        return copy(latc.at[(y + d) % 4], latr.at[y], LAT_Y + d, (s, tok(y + d, l)))

    def spread_latents():
        for yy in range(4):
            for zz in range(4):
                first = zz * COLS + yy * PIECE
                latc[yy, :, zz * PIECE:(zz + 1) * PIECE] = lat[:, first:first + PIECE]
        latr[y] = latc[y]

    pl.when(c == 1)(spread_latents)

    tm, tp, tx = tok(y + 3, l), tok(y + 1, l), tok(y, 1 - l)
    t2 = tok(y + 2, l)
    um, up, u2 = tok(y + 3, 1 - l), tok(y + 1, 1 - l), tok(y + 2, 1 - l)

    @pl.when(gather)
    def _():
        for d in range(1, 4):
            src = wot.at[ocols(z), lanes(0)]
            copy(src, src, SEM["o_a0"] + d, YP).wait_recv()
        o_copy("o_xh", XH, z).start()

    t_x.append(send(shard(t, 1), "t_x1", XL))
    t_yp[0].wait_recv()
    t_fp = send(shard(tm, 0), "t_fp", YP)
    w_zp0.wait_recv()
    pm = slot(z + 3, h, c)
    w_fp0 = send(wrows(pm, 0, PIECE // 2), "w_fp0", ZP)
    w_co.append(send(wrows(pm), "w_co2", CO))
    w_zm0.wait_recv()
    pp = slot(z + 1, h, c)
    w_fm0 = send(wrows(pp, PIECE // 2, PIECE // 2), "w_fm0", ZM)
    w_co.append(send(wrows(pp), "w_co3", CO))
    w_xh.wait_recv()
    px = slot(z, 1 - h, c)
    w_zp1 = send(wrows(px), "w_zp1", ZP)
    w_zm1 = send(wrows(px), "w_zm1", ZM)
    w_co.append(send(wrows(px), "w_co1", CO))
    u_yp, u_ym = [], []

    def second(half):
        t_x[half].wait_recv()
        u_yp.append(send(shard(tx, half), "u_yp%d" % half, YP))
        u_ym.append(send(shard(tx, half), "u_ym%d" % half, YM))

    second(0)
    t_ym[1].wait_recv()
    t_fm = send(shard(tp, 1), "t_fm", YM)
    second(1)

    w_zp1.wait_recv()
    pm1 = slot(z + 3, 1 - h, c)
    w_fp1 = send(wrows(pm1, 0, PIECE // 2), "w_fp1", ZP)
    w_co.append(send(wrows(pm1), "w_co4", CO))
    w_zm1.wait_recv()
    pp1 = slot(z + 1, 1 - h, c)
    w_fm1 = send(wrows(pp1, PIECE // 2, PIECE // 2), "w_fm1", ZM)
    w_co.append(send(wrows(pp1), "w_co5", CO))

    def spread():
        for name, dev in (("o_zp", ZP), ("o_zm", ZM), ("o_co0", CO)):
            o_copy(name, dev, z).start()

    @pl.when(relay)
    def _():
        o_copy("o_xh", XH, z).wait_recv()

    @pl.when(active)
    def _():
        spread()

    w_fp0.wait_recv()
    w_fm0.wait_recv()
    w_co.append(send(wrows(slot(z + 2, h, c)), "w_co6", CO))
    t_fm.wait_recv()
    u_x = send(shard(t2, 1), "u_x", XL)

    w_fp1.wait_recv()
    w_fm1.wait_recv()
    w_co.append(send(wrows(slot(z + 2, 1 - h, c)), "w_co7", CO))
    for cp in w_co:
        cp.wait_recv()

    def quarter(tt, part):
        return x.at[tt, pl.ds(part * 32, 32)]

    def u_forward():
        a, b = quarter(um, 0), quarter(up, 1)
        return copy(a, a, "u_fp", YP), copy(b, b, "u_fm", YM)

    def kv_copy(tt, half, k):
        rows = pl.ds(pl.multiple_of(half * HALF, HALF), HALF)
        return copy(ctx.at[tt, rows], ctx.at[8 + tt, rows], KV0 + k, NX)

    def project(b, _):
        @pl.when(b == 1)
        def _():
            @pl.when(active)
            def _():
                o_copy("o_zm", ZM, z + 1).wait_recv()
                o_copy("o_z2", ZM, z + 1).start()
                o_copy("o_co2", CO, z + 1).start()

            t_yp[1].wait_recv()
            t_ym[0].wait_recv()

        @pl.when(b == 2)
        def _():
            t_fp.wait_recv()

        def pick(values):
            return jnp.where(b == 0, values[0], jnp.where(b == 1, values[1], values[2]))

        parts = [
            (pick((t, tm, um)), 0),
            (pick((t, tm, up)), pick((1, 1, 0))),
            (pick((tx, tp, t2)), 0),
            (pick((tx, tp, t2)), 1),
        ]
        compute(parts, 4 * b)
        return 0

    def compute(parts, first):
        parts = [(tt, half, pl.ds(pl.multiple_of(half * HALF, HALF), HALF)) for tt, half in parts]
        rows = jnp.concatenate([x[tt, rr, :] for tt, half, rr in parts], axis=0)
        for n in range(3):
            cols = slice(n * NTILE, (n + 1) * NTILE)
            part = jnp.dot(rows, w[:, GROUP + n * NTILE:GROUP + (n + 1) * NTILE], preferred_element_type=F32).astype(BF16)
            for i, (tt, half, rr) in enumerate(parts):
                ctx[tt, rr, cols] = part[i * HALF:(i + 1) * HALF]
        for i, (tt, half, rr) in enumerate(parts):
            kv_copy(tt, half, first + i).start()
        part = jnp.dot(rows, w[:, :GROUP], preferred_element_type=F32).astype(BF16)
        for i, (tt, half, rr) in enumerate(parts):
            q[tt, rr, :] = part[i * HALF:(i + 1) * HALF]

    u_yp[0].wait_recv()
    u_ym[0].wait_recv()
    for cp in u_forward():
        cp.start()

    @pl.when(c == 1)
    def _():
        for d in (1, 3, 2):
            lat_copy(d).start()

    lax.fori_loop(0, 3, project, 0)
    u_yp[1].wait_recv()
    u_ym[1].wait_recv()
    u_x.wait_recv()
    compute([(um, 1), (up, 1), (u2, 1)], 12)
    for cp in u_forward():
        cp.wait_recv()
    compute([(u2, 0)], 15)

    @pl.when(active)
    def _():
        for name, dz, onward in (("o_zp", 3, "o_co1"), ("o_z2", 2, "o_co3")):
            o_copy(name, ZP, z + dz).wait_recv()
            o_copy(onward, CO, z + dz).start()

    for k in range(16):
        kv_copy(t, 0, k).wait_recv()


    scale = 1.0 / math.sqrt(HD)

    def tile_at(yt, second_half):
        return 2 * (yt % 4) + jnp.where(second_half, here, 1 - here)

    def a_copy(j, late, base):
        if base == A_YP:
            ref, dev = att.at[tile_at(y + 1 + j, late), :, lanes(y)], YP
        elif base == A_YM:
            ref, dev = att.at[tile_at(y + 1 + j, late), :, lanes(y)], YM
        elif base == A_FP:
            ref, dev = att.at[tile_at(y + j, late), pl.ds(0, HALF), lanes(y + 3)], YP
        else:
            ref, dev = att.at[tile_at(y + 2 + j, late), pl.ds(HALF, HALF), lanes(y + 1)], YM
        return copy(ref, ref, base + j + jnp.where(late, 4, 0), dev)

    def at(k, values):
        return jnp.where(k == 0, values[0], jnp.where(k == 1, values[1], jnp.where(k == 2, values[2], values[3])))

    def attend(i):
        listed = [ids[j, i] for j in range(4)]
        valid = []
        for j in range(4):
            ok = j < counts[i]
            for e in range(j):
                ok = ok & (listed[e] != listed[j])
            valid.append(ok)
        outs = []
        ones = jnp.ones((4 * BLK, HD), BF16)
        for head in range(3):
            hc = slice(head * HD, (head + 1) * HD)
            vc = slice(GROUP + head * HD, GROUP + (head + 1) * HD)
            keys = jnp.concatenate([ctx[listed[j], :, hc] for j in range(4)], axis=0)
            scores = lax.dot_general(q[i, :, hc], keys, (((1,), (1,)), ((), ())), preferred_element_type=F32)
            scores = [jnp.where(valid[j], scores[:, j * BLK:(j + 1) * BLK], -1e30) for j in range(4)]
            top = jnp.maximum(jnp.maximum(scores[0], scores[1]), jnp.maximum(scores[2], scores[3]))
            top = jnp.max(top, axis=1, keepdims=True)
            probs = jnp.concatenate([jnp.exp((sc - top) * scale).astype(BF16) for sc in scores], axis=1)
            values = jnp.concatenate([ctx[listed[j], :, vc] for j in range(4)], axis=0)
            sums = jnp.dot(probs, jnp.concatenate([values, ones], axis=1), preferred_element_type=F32)
            outs.append((sums[:, :HD] / sums[:, HD:]).astype(BF16))
        att[i, :, lanes(y)] = jnp.concatenate(outs, axis=1)

    def onward_p(j, late):
        a_copy(j, late, A_YP).wait_recv()
        a_copy(j, late, A_FP).start()

    def onward_m(j, late):
        a_copy(j, late, A_YM).wait_recv()
        a_copy(j, late, A_FM).start()

    def attention(k, _):
        late = k >= 4
        attend(tile_at(y + 1 + at(k % 4, ORDER), late))

        @pl.when(k == 0)
        def _():
            a_copy(2, False, A_YP).start()
            a_copy(2, False, A_YM).start()

        @pl.when(k == 1)
        def _():
            a_copy(1, False, A_YP).start()

        @pl.when(k == 2)
        def _():
            a_copy(3, False, A_YM).start()

        @pl.when(k == 5)
        def _():
            onward_p(2, False)
            onward_m(2, False)
            a_copy(3, False, A_YP).start()
            a_copy(0, False, A_YM).start()
            a_copy(0, False, A_YP).start()
            a_copy(1, False, A_YM).start()

        return 0

    lax.fori_loop(0, 8, attention, 0)

    CORE = ("o_co0", "o_co1", "o_co2", "o_co3")

    @pl.when(jnp.logical_not(active))
    def _():
        for name in CORE:
            o_copy(name, CO, z).wait_recv()

    def turn(r, _):
        rows = pl.ds(pl.multiple_of(r * 128, 128), 128)
        wout[:, rows] = wot[rows, :].T
        return 0

    lax.fori_loop(0, 10, turn, 0)

    def product(p, late):
        j = (p + 2) % 4
        a_copy(j, late, A_FP).wait_recv()
        a_copy(j, late, A_FM).wait_recv()
        return jnp.dot(att[tile_at(y + 1 + p, late)], wout[...], preferred_element_type=F32)

    def p_copy(p):
        return copy(psend.at[p], precv.at[p], P_X + p, XL)

    def foreign(p):
        mine = product(p, False)

        @pl.when(c == 0)
        def _():
            psend[p] = mine.astype(BF16)

        @pl.when(c == 1)
        def _():
            psend[p] = (mine + latr[(y + 1 + p) % 4].astype(F32)).astype(BF16)

        p_copy(p).start()

    def late_sends(*tiles):
        for j in tiles:
            a_copy(j, True, A_YP).start()
            a_copy(j, True, A_YM).start()

    @pl.when(c == 1)
    def _():
        for d in (1, 2, 3):
            lat_copy(d).wait_recv()

    onward_p(1, False)
    onward_m(3, False)
    foreign(0)
    onward_p(3, False)
    onward_m(0, False)
    late_sends(2, 1)
    foreign(1)
    onward_p(0, False)
    onward_m(1, False)
    late_sends(3, 0)
    foreign(2)
    foreign(3)
    for j in ORDER:
        onward_p(j, True)
        onward_m(j, True)

    def s_copy(p):
        return copy(ssend.at[p], branch.at[y], S_Y + p, (NX[0], tok(y + 1 + p, here)))

    def finish(p, _):
        mine = product(p, True)
        p_copy(p).wait_recv()
        ssend[p] = (mine + precv[p].astype(F32)).astype(BF16)
        s_copy(p).start()
        return 0

    lax.fori_loop(0, 4, finish, 0)

    for cp in sent:
        if cp is not t_yp[0]:
            cp.wait_send()

    @pl.when(c == 0)
    def _():
        t_yp[0].wait_send()

    for cp in u_forward():
        cp.wait_send()

    def drain(k, _):
        kv_copy(t, 0, 2 * k).wait_send()
        kv_copy(t, 0, 2 * k + 1).wait_send()
        for base in (A_YP, A_YM, A_FP, A_FM):
            a_copy(k % 4, k >= 4, base).wait_send()
        return 0

    lax.fori_loop(0, 8, drain, 0)
    for p in range(4):
        p_copy(p).wait_send()
        s_copy(p).wait_send()

    @pl.when(c == 0)
    def _():
        copy(lat, lat_prev, LAT, NX).wait_send()

    @pl.when(c == 1)
    def _():
        for d in (1, 2, 3):
            lat_copy(d).wait_send()


    @pl.when(jnp.logical_not(gather))
    def _():
        o_first().wait_send()

    @pl.when(gather)
    def _():
        o_copy("o_xh", XH, z).wait_send()

    @pl.when(active)
    def _():
        for name in ("o_zp", "o_zm", "o_z2") + CORE:
            o_copy(name, CO, z).wait_send()


    @pl.when(c == 1)
    def _():
        copy(lat, lat_prev, LAT, NX).wait_recv()

    for p in range(4):
        s_copy(p).wait_recv()


def residual(branch, lat, out):
    add = lax.axis_index("slot") % 2 == 1
    for zz in range(4):
        cols = slice(zz * COLS, (zz + 1) * COLS)
        pieces = [branch[yy, :, zz * PIECE:(zz + 1) * PIECE] for yy in range(4)]
        base = jnp.where(add, lat[:, cols].astype(F32), 0.0)
        out[:, cols] = (base + jnp.concatenate(pieces, axis=1).astype(F32)).astype(BF16)


def body(latents, gain, mod_table, slot_noise_level, key_block_index, counts, w_qkv, w_out):
    vmem = pl.BlockSpec(memory_space=pltpu.VMEM)
    smem = pl.BlockSpec(memory_space=pltpu.SMEM)
    hbm = pl.BlockSpec(memory_space=pl.ANY)
    blocks = pltpu.VMEM((4, ROWS, COLS), BF16)
    branch, lat_prev = pl.pallas_call(
        kernel,
        out_shape=[jax.ShapeDtypeStruct((4, ROWS, COLS), BF16), jax.ShapeDtypeStruct((ROWS, D), BF16)],
        in_specs=[hbm, vmem, hbm, smem, smem, smem, hbm, hbm],
        out_specs=[hbm, hbm],
        scratch_shapes=[
            pltpu.VMEM((8, ROWS, D), BF16),
            pltpu.VMEM((D, QKV), BF16),
            pltpu.VMEM((COLS, 4 * GROUP), BF16),
            pltpu.VMEM((4 * GROUP, COLS), BF16),
            pltpu.VMEM((8, ROWS, GROUP), BF16),
            pltpu.VMEM((16, ROWS, 2 * GROUP), BF16),
            pltpu.VMEM((8, ROWS, 4 * GROUP), BF16),
            blocks,
            blocks,
            blocks,
            blocks,
            blocks,
            pltpu.VMEM((ROWS, D), BF16),
            pltpu.VMEM((16, 2, D), F32),
            pltpu.SemaphoreType.DMA((6,)),
            pltpu.SemaphoreType.REGULAR,
            pltpu.SemaphoreType.DMA((N_SEM,)),
            pltpu.SemaphoreType.DMA((N_SEM,)),
        ],
        compiler_params=pltpu.CompilerParams(
            collective_id=0, has_side_effects=True, vmem_limit_bytes=60 * 2**20
        ),
        name="window",
    )(latents[0], gain[None], mod_table, slot_noise_level, key_block_index[0].T, counts[0], w_qkv, w_out.T)
    out = pl.pallas_call(
        residual,
        grid=(2,),
        out_shape=jax.ShapeDtypeStruct((ROWS, D), BF16),
        in_specs=[pl.BlockSpec((4, ROWS // 2, COLS), lambda i: (0, i, 0)), pl.BlockSpec((ROWS // 2, D), lambda i: (i, 0))],
        out_specs=pl.BlockSpec((ROWS // 2, D), lambda i: (i, 0)),
        name="residual",
    )(branch, lat_prev)
    return out[None]


def solution(mesh):
    in_specs = (
        P("slot", "tok", None),
        P(),
        P(),
        P("slot"),
        P("slot", None, None),
        P("slot", None),
        P(None, "slot", "tok"),
        P("tok", "slot"),
    )
    out_specs = P("slot", "tok", None)
    return jax.shard_map(body, mesh=mesh, in_specs=in_specs, out_specs=out_specs, check_vma=False)
```
